256 devices in a mesh: seq: 32 (over z_lo, y, core), kv: 8 (over x, z_hi).
Axes of the slice: x: 4, y: 4, z: 8 (z_hi: 2, z_lo: 4; z = z_hi * 4 + z_lo), core: 2. Of those that a mesh axis runs over, the one named last changes fastest.
Arguments:
- queries: bfloat16 [16384, 4096], P('seq', 'kv'), may hold values from -20 to 20
- key_rows: bfloat16 [16384, 1024], P('seq', 'kv'), may hold values from -6 to 6
- value_rows: bfloat16 [16384, 1024], P('seq', 'kv'), may hold values from -6 to 6
- out_weight: bfloat16 [4096, 4096], P('kv', 'seq'), may hold values from -0.1875 to 0.1875
- vertical: int32 [32, 16], replicated, may hold values from 0 to 126, all different within a row
- slash_offsets: int32 [32, 16], replicated, may hold values from 0 to 510
Outputs:
- projected: bfloat16 [16384, 4096], P('seq', 'kv')
The draws below stay inside these ranges and needn't reach their ends.
Inputs may be any that keep to these rules, and one draw needn't show every extreme that they name: `vertical`: each row lists distinct entries.
All inputs are finite; a program needn't handle non-finite values.
Results may differ from the reference program's by a relative error of at most 0.015.
Values may be sent and summed in bfloat16 or wider, within the bound.
A program may use at most 128 MiB of HBM per device.

```python
import math
import jax
import jax.numpy as jnp
from jax import lax

D = 4096
HEAD_DIM = 128
GROUP = 4
BLOCK = 128
NV = 16
NS = 16
Q_DEV = 512
KV_HEADS = 8
HEADS = 32
TOKENS = 16384
NB = 128
N_SEQ = 32


def draw_queries(key, part):
    key = jax.random.fold_in(key, 11)
    shape = (TOKENS, HEADS * HEAD_DIM)
    base = jnp.clip(jax.random.normal(key, shape, jnp.float32), -6.0, 6.0)
    return base.astype(jnp.bfloat16)


def draw_key_rows(key, part):
    key = jax.random.fold_in(key, 13)
    shape = (TOKENS, KV_HEADS * HEAD_DIM)
    base = jnp.clip(jax.random.normal(key, shape, jnp.float32), -6.0, 6.0)
    return base.astype(jnp.bfloat16)


def draw_slash_offsets(key, part):
    key = jax.random.fold_in(key, 17)
    entries = jax.random.randint(key, (HEADS, NS), 0, Q_DEV - 1)
    chosen = jax.random.randint(jax.random.fold_in(key, 3), (2,), 0, HEADS)
    entries = entries.at[chosen[0], 0].set(Q_DEV - 2)
    entries = entries.at[chosen[1], 1].set(0)
    return entries.astype(jnp.int32)


def raised(drawn, rng, source, target, shards_of, factor):
    def block_of(axis_at):
        return (jnp.arange(drawn.shape[axis_at]) // (drawn.shape[axis_at] // shards_of)).reshape((-1,) + (1,) * (drawn.ndim - 1 - axis_at))

    one_side = jax.random.permutation(rng, shards_of)[block_of(target)]
    other_side = (block_of(target) + shards_of // 2) % shards_of
    return jnp.where((block_of(source) == one_side) | (block_of(source) == other_side), factor * drawn, drawn)


def level_of(stream_key, extent, pieces, least, top_value):
    def one(axis_at, blocks):
        heights = jax.random.uniform(jax.random.fold_in(jax.random.fold_in(stream_key, 6), axis_at), (blocks,), jnp.float32, least / len(pieces), top_value / len(pieces))
        return jnp.repeat(jnp.exp(heights), extent[axis_at] // blocks).reshape((-1,) + (1,) * (len(extent) - axis_at - 1))

    factor_of = one(*pieces[0])
    for cut in pieces[1:]:
        factor_of = factor_of * one(*cut)
    return factor_of


def choose_distinct(key, rows, amount, top, lift):
    ranking = jax.random.permutation(jax.random.fold_in(key, 1), amount)
    boost = ranking
    for power in range(3):
        boost = boost * boost // amount
    boost = boost * lift // amount
    chance = jax.random.randint(jax.random.fold_in(key, 2), (rows, amount), 0, 4096) + boost
    fixed_rows = jax.random.permutation(jax.random.fold_in(key, 3), rows)[jnp.arange(amount) % rows]
    chance = jnp.where(jnp.arange(rows)[:, None] == fixed_rows[None, :], 1 << 14, chance)
    merit = chance * amount + jnp.arange(amount)
    return lax.top_k(merit.astype(jnp.int32), top)[1].astype(jnp.int32)


def scatter_about(rng, dims, width, limit, shards=(), held_as=jnp.bfloat16):
    values = width * jax.random.normal(rng, dims, jnp.float32)
    if shards:
        values = values * level_of(rng, dims, shards, -0.22, 0.18)
    return jnp.clip(values, -limit, limit).astype(held_as)


def noise_with(rng, extent, spread, limit, shards, heavy, held_as=jnp.bfloat16):
    result = spread * jax.random.normal(rng, extent, jnp.float32)
    if shards:
        result = result * level_of(rng, extent, shards, -0.22, 0.18)
    return jnp.clip(raised(result, jax.random.fold_in(rng, 3), *heavy), -limit, limit).astype(held_as)


def setup_inputs(seed: int = 0) -> dict:
    arg_keys = jax.random.split(jax.random.key(seed), 7)
    queries = draw_queries(jax.random.fold_in(arg_keys[6], 71), 0)
    key_rows = draw_key_rows(jax.random.fold_in(arg_keys[6], 71), 0)
    value_rows = scatter_about(arg_keys[2], (TOKENS, KV_HEADS * HEAD_DIM), 1.0, 6.0, ((0, 32), (1, 8)))
    out_weight = noise_with(arg_keys[3], (HEADS * HEAD_DIM, D), (HEADS * HEAD_DIM) ** -0.5, 0.1875, ((0, 8), (1, 32)), (0, 1, 32, 2.75))
    vertical = choose_distinct(arg_keys[4], HEADS, NB - 1, NV, 0)
    slash_offsets = draw_slash_offsets(jax.random.fold_in(arg_keys[6], 71), 0)
    return {"queries": queries, "key_rows": key_rows, "value_rows": value_rows, "out_weight": out_weight, "vertical": vertical, "slash_offsets": slash_offsets}


def attend(query_head, window_key, window_value, picked_key, picked_value, offsets, column_ids, first_row):
    length = query_head.shape[0]
    factor = 1.0 / math.sqrt(query_head.shape[1])
    window_scores = jnp.dot(query_head, window_key.T, preferred_element_type=jnp.float32) * factor
    picked_scores = jnp.dot(query_head, picked_key.T, preferred_element_type=jnp.float32) * factor
    query_pos = first_row + jnp.arange(length, dtype=jnp.int32)
    key_pos = first_row - length + jnp.arange(2 * length, dtype=jnp.int32)
    distance = query_pos[:, None] - key_pos[None, :]
    on_slash = (distance == 0) | jnp.any(distance[:, :, None] == (offsets + 1)[None, None, :], axis=-1)
    on_column = jnp.any((key_pos // BLOCK)[:, None] == column_ids[None, :], axis=-1)
    earlier_column = on_column & (key_pos < first_row)
    window_mask = (key_pos >= 0)[None, :] & (distance >= 0) & (on_slash | on_column[None, :]) & (~earlier_column)[None, :]
    keep_block = column_ids < first_row // BLOCK
    picked_mask = jnp.repeat(keep_block, BLOCK)[None, :]
    window_scores = jnp.where(window_mask, window_scores, -jnp.inf)
    picked_scores = jnp.where(picked_mask, picked_scores, -jnp.inf)
    row_peak = jnp.maximum(lax.optimization_barrier(jnp.max(window_scores, axis=1)), lax.optimization_barrier(jnp.max(picked_scores, axis=1)))[:, None]
    window_prob = jnp.exp(window_scores - row_peak)
    picked_prob = jnp.exp(picked_scores - row_peak)
    denominator = lax.optimization_barrier(jnp.sum(window_prob, axis=1)) + lax.optimization_barrier(jnp.sum(picked_prob, axis=1))
    mixed = jnp.dot(window_prob.astype(jnp.bfloat16), window_value, preferred_element_type=jnp.float32)
    mixed = mixed + jnp.dot(picked_prob.astype(jnp.bfloat16), picked_value, preferred_element_type=jnp.float32)
    return mixed / denominator[:, None]

def reference(queries, key_rows, value_rows, out_weight, vertical, slash_offsets):
    column_all = jnp.concatenate([jnp.zeros((HEADS, 1), jnp.int32), vertical.astype(jnp.int32) + 1], axis=1)
    query_heads = queries.reshape(TOKENS, HEADS, HEAD_DIM)
    key_heads = key_rows.reshape(TOKENS, KV_HEADS, HEAD_DIM)
    value_heads = value_rows.reshape(TOKENS, KV_HEADS, HEAD_DIM)
    padding = jnp.zeros((Q_DEV, KV_HEADS, HEAD_DIM), jnp.bfloat16)
    padded_keys = jnp.concatenate([padding, key_heads], axis=0)
    padded_values = jnp.concatenate([padding, value_heads], axis=0)
    key_blocks = key_heads.reshape(NB, BLOCK, KV_HEADS, HEAD_DIM)
    value_blocks = value_heads.reshape(NB, BLOCK, KV_HEADS, HEAD_DIM)
    weights = out_weight.reshape(KV_HEADS, GROUP * HEAD_DIM, D).astype(jnp.float32)

    def one_block(block_index):
        first_row = block_index * Q_DEV
        block_queries = lax.dynamic_slice_in_dim(query_heads, first_row, Q_DEV, 0)
        window_key = lax.dynamic_slice_in_dim(padded_keys, first_row, 2 * Q_DEV, 0)
        window_value = lax.dynamic_slice_in_dim(padded_values, first_row, 2 * Q_DEV, 0)

        def one_head(head_index):
            group_index = head_index // GROUP
            block_ids = column_all[head_index]
            picked_key = jnp.take(key_blocks, block_ids, axis=0)[:, :, group_index].reshape(-1, HEAD_DIM)
            picked_value = jnp.take(value_blocks, block_ids, axis=0)[:, :, group_index].reshape(-1, HEAD_DIM)
            return attend(block_queries[:, head_index], window_key[:, group_index], window_value[:, group_index], picked_key, picked_value, slash_offsets[head_index], block_ids, first_row)
        per_head = lax.map(one_head, jnp.arange(HEADS, dtype=jnp.int32))
        attention = jnp.transpose(per_head, (1, 0, 2)).reshape(Q_DEV, HEADS * HEAD_DIM).astype(jnp.bfloat16)
        grouped = attention.reshape(Q_DEV, KV_HEADS, GROUP * HEAD_DIM).astype(jnp.float32)
        partial_sums = jnp.einsum('qgk,gkd->gqd', grouped, weights).astype(jnp.bfloat16)
        partial_sums = lax.optimization_barrier(partial_sums)
        return lax.optimization_barrier(jnp.sum(partial_sums.astype(jnp.float32), axis=0)).astype(jnp.bfloat16)
    outputs = lax.map(one_block, jnp.arange(N_SEQ, dtype=jnp.int32))
    return outputs.reshape(TOKENS, D)
```

```python
import functools
import math

import jax
import jax.numpy as jnp
from jax import lax
from jax.experimental import pallas as pl
from jax.experimental.pallas import tpu as pltpu
from jax.sharding import PartitionSpec as P

MESH = pl.DeviceIdType.MESH
HEAD_DIM = 128
BLOCK = 128
GROUP = 4
ROWS = 512
NV = 16
NS = 16
NPICK = NV + 1
RBLK = ROWS // BLOCK
WIN = 5 * BLOCK
PICK = NPICK * BLOCK
NEG = -1e30
SCALE = math.log2(math.e) / math.sqrt(HEAD_DIM)


def dot(a, b):
    return jnp.dot(a, b, preferred_element_type=jnp.float32)


def dot_t(a, b):
    return lax.dot_general(a, b, (((1,), (1,)), ((), ())), preferred_element_type=jnp.float32)


def kernel(
    vert, slash, q_ref, k_hbm, v_hbm, w_hbm, out_ref,
    kvbuf, wbuf, abuf, kcat, vcat, sbias, own, zsrc, relay, zdst,
    lsem, zs, zr, ys, yr, ys2, yr2, cs, cr,
    wxs, wxr, wzs, wzr, wys, wyr, wys2, wyr2, wcs, wcr,
    xs, xr, xs2, xr2, es, er, fs, fr,
):
    seq = lax.axis_index("seq")
    kv = lax.axis_index("kv")
    core = seq % 2
    y = (seq // 2) % 4
    p = seq // 8
    x = kv // 2
    zh = kv % 2
    z = zh * 4 + p

    def dev(x_, y_, z_, c_):
        return (((z_ % 4) * 4 + y_) * 2 + c_, x_ * 2 + z_ // 4)

    sib = dev(x, y, z, 1 - core)
    y_to = [dev(x, (y + 1) % 4, z, core), dev(x, (y + 3) % 4, z, core)]
    z_up = dev(x, y, (z + 1) % 8, core)
    z_dn = dev(x, y, (z + 7) % 8, core)
    z_two = [dev(x, y, (z + 2) % 8, core), dev(x, y, (z + 6) % 8, core)]
    x_to = [dev((x + 1) % 4, y, z, core), dev((x + 3) % 4, y, z, core)]
    x_far = dev((x + 2) % 4, y, z, core)

    def rc(src, dst, ss, rs, d):
        return pltpu.make_async_remote_copy(
            src_ref=src, dst_ref=dst, send_sem=ss, recv_sem=rs, device_id=d, device_id_type=MESH
        )

    def chunk(q, yy, c):
        return kvbuf.at[pl.ds(4 + 4 * ((q * 4 + yy) * 2 + c), 4)]

    def half(q, yy, c, h):
        return kvbuf.at[pl.ds(4 + 4 * ((q * 4 + yy) * 2 + c) + 2 * h, 2)]

    base = 4 + 4 * seq
    copies = [
        pltpu.make_async_copy(k_hbm, kvbuf.at[pl.ds(base, 4), 0], lsem.at[0]),
        pltpu.make_async_copy(v_hbm, kvbuf.at[pl.ds(base, 4), 1], lsem.at[1]),
    ]
    for c in copies:
        c.start()
    w_local = pltpu.make_async_copy(w_hbm, wbuf.at[y, core, x], lsem.at[2])

    @pl.when(x == p)
    def _():
        w_local.start()

    barrier = pltpu.get_barrier_semaphore()
    partners = [sib, *y_to, z_up, z_dn, *z_two, *x_to, x_far]
    for d in partners:
        pl.semaphore_signal(barrier, inc=1, device_id=d, device_id_type=MESH)
    for c in copies:
        c.wait()
    pl.semaphore_wait(barrier, len(partners))

    def z_send(t):
        return rc(chunk(p - t, y, core), chunk(p - t, y, core), zs.at[t], zr.at[t + 1], z_up)

    def y_send(t, d):
        return rc(chunk(p - t, y, core), chunk(p - t, y, core), ys.at[d, t], yr.at[d, t], y_to[d])

    def y_got(t, d):
        c = chunk(p - t, (y + 3 - 2 * d) % 4, core)
        return rc(c, c, ys.at[d, t], yr.at[d, t], y_to[d])

    def y_next(t, d):
        c = half(p - t, (y + 3 - 2 * d) % 4, core, d)
        return rc(c, c, ys2.at[d, t], yr2.at[d, t], y_to[d])

    def y_far(t, d):
        c = half(p - t, (y + 2) % 4, core, d)
        return rc(c, c, ys2.at[d, t], yr2.at[d, t], y_to[d])

    def c_send(t, off):
        c = chunk(p - t, (y + off) % 4, core)
        return rc(c, c, cs.at[t, off], cr.at[t, off], sib)

    def c_got(t, off):
        c = chunk(p - t, (y + off) % 4, 1 - core)
        return rc(c, c, cs.at[t, off], cr.at[t, off], sib)

    def enter(t):
        @pl.when(p >= t)
        def _():
            if t > 0:
                c = chunk(p - t, y, core)
                rc(c, c, zs.at[t], zr.at[t], z_up).wait_recv()
            if t < 3:
                @pl.when(p < 3)
                def _():
                    z_send(t).start()
            for d in range(2):
                y_send(t, d).start()
            c_send(t, 0).start()

    def onward(t):
        @pl.when(p >= t)
        def _():
            for d in range(2):
                y_got(t, d).wait_recv()
                y_next(t, d).start()
                c_send(t, 3 - 2 * d).start()

    def finish(t):
        @pl.when(p >= t)
        def _():
            for d in range(2):
                y_far(t, d).wait_recv()
            c_send(t, 2).start()

    def w_move():
        return rc(w_hbm, wbuf.at[y, core, x], wxs.at[0], wxr.at[x], dev(p, y, z, core))

    def wz_send(i, d):
        c = wbuf.at[y, core, i]
        return rc(c, c, wzs.at[d, i], wzr.at[i], z_up if d == 0 else z_dn)

    def w_pass(i):
        c = wbuf.at[y, core, i]

        @pl.when((x == p) & (x != i))
        def _():
            rc(c, c, wxs.at[0], wxr.at[i], sib).wait_recv()

        @pl.when(x != p)
        def _():
            rc(c, c, wzs.at[0, i], wzr.at[i], sib).wait_recv()

        @pl.when((p >= x) & (p < 3))
        def _():
            wz_send(i, 0).start()

        @pl.when((p <= x) & (p > 0))
        def _():
            wz_send(i, 1).start()

    def wy(yy, d, ss, rs):
        c = wbuf.at[yy, core]
        return rc(c, c, ss, rs, y_to[d])

    def wy_half(yy, d):
        c = wbuf.at[yy, core, pl.ds(2 * d, 2)]
        return rc(c, c, wys2.at[d], wyr2.at[d], y_to[d])

    def wc(off, c_):
        c = wbuf.at[(y + off) % 4, c_]
        return rc(c, c, wcs.at[off], wcr.at[off], sib)

    @pl.when(x != p)
    def _():
        w_move().start()

    enter(0)

    kvbuf[0:4] = jnp.zeros((4, 2, BLOCK, HEAD_DIM), jnp.bfloat16)

    def mask_step(n, carry):
        m, strip = n // 4, n % 4
        i = lax.broadcasted_iota(jnp.int32, (32, WIN), 0) + strip * 32
        j = lax.broadcasted_iota(jnp.int32, (32, WIN), 1)
        d = 4 * BLOCK + i - j
        b = jnp.where(d == 0, 0.0, NEG)
        for e in range(NS):
            b = jnp.where(d == slash[kv * GROUP + m, e] + 1, 0.0, b)
        sbias[m, pl.ds(pl.multiple_of(strip * 32, 32), 32), :] = b
        return carry

    lax.fori_loop(0, 16, mask_step, 0)

    enter(1)
    onward(0)
    enter(2)
    onward(1)
    finish(0)
    enter(3)
    onward(2)
    finish(1)

    @pl.when(x == p)
    def _():
        w_local.wait()

    for i in range(4):
        w_pass(i)
    onward(3)
    finish(2)
    finish(3)
    for t in range(4):
        @pl.when(p >= t)
        def _(t=t):
            for off in range(4):
                c_got(t, off).wait_recv()

    for d in range(2):
        wy(y, d, wys.at[d], wyr.at[d]).start()
    wc(0, core).start()

    def gather(m, carry):
        for j in range(NPICK):
            b = 0 if j == 0 else vert[kv * GROUP + m, j - 1] + 1
            at = 4 + (0 if j == 0 else jnp.where(b < 4 * seq + 4, b, 0))
            kcat[m, j * BLOCK : (j + 1) * BLOCK, :] = kvbuf[at, 0]
            vcat[m, j * BLOCK : (j + 1) * BLOCK, :] = kvbuf[at, 1]
        return carry

    lax.fori_loop(0, GROUP, gather, 0)

    wi = lax.broadcasted_iota(jnp.int32, (BLOCK, WIN), 0)
    wj = lax.broadcasted_iota(jnp.int32, (BLOCK, WIN), 1)
    lane = lax.broadcasted_iota(jnp.int32, (1, WIN), 1)

    def attend(r):
        rows = pl.ds(pl.multiple_of(r * BLOCK, BLOCK), BLOCK)
        here = 4 * seq + r
        for m in range(GROUP):
            cols = slice(m * HEAD_DIM, (m + 1) * HEAD_DIM)
            q = q_ref[rows, cols]
            kw = kvbuf[pl.ds(here, 5), 0].reshape(WIN, HEAD_DIM)
            vw = kvbuf[pl.ds(here, 5), 1].reshape(WIN, HEAD_DIM)
            bcol = here - 4 + lane // BLOCK
            oncol = bcol <= 0
            pb = [jnp.full((1, BLOCK), jnp.where(here > 0, 0.0, NEG), jnp.float32)]
            for e in range(NV):
                b = vert[kv * GROUP + m, e] + 1
                oncol = oncol | (bcol == b)
                pb.append(jnp.full((1, BLOCK), jnp.where(b < here, 0.0, NEG), jnp.float32))
            alt = jnp.where((wj >= 4 * BLOCK) & (wi >= wj - 4 * BLOCK), 0.0, NEG)
            bias = jnp.where(oncol, alt, sbias[m])
            sw = dot_t(q, kw) + bias
            sp = dot_t(q, kcat[m]) + jnp.concatenate(pb, axis=1)
            peak = jnp.maximum(
                jnp.max(sw, axis=1, keepdims=True), jnp.max(sp, axis=1, keepdims=True)
            )
            pw = jnp.exp2((sw - peak) * SCALE).astype(jnp.bfloat16)
            pp = jnp.exp2((sp - peak) * SCALE).astype(jnp.bfloat16)
            ones_w = jnp.ones((WIN, HEAD_DIM), jnp.bfloat16)
            ones_p = jnp.ones((PICK, HEAD_DIM), jnp.bfloat16)
            o = dot(pw, jnp.concatenate([vw, ones_w], axis=1))
            o = o + dot(pp, jnp.concatenate([vcat[m], ones_p], axis=1))
            abuf[x, rows, cols] = (o[:, :HEAD_DIM] / o[:, HEAD_DIM:]).astype(jnp.bfloat16)

    def a_part(xx, r):
        return abuf.at[xx, pl.ds(pl.multiple_of(r * BLOCK, BLOCK), BLOCK)]

    def a_half(xx, r, d):
        return abuf.at[xx, pl.ds(pl.multiple_of(r * BLOCK + d * 64, 64), 64)]

    def x_send(r, d):
        return rc(a_part(x, r), a_part(x, r), xs.at[d, r], xr.at[d, r], x_to[d])

    def x_got(r, d):
        c = a_part((x + 3 - 2 * d) % 4, r)
        return rc(c, c, xs.at[d, r], xr.at[d, r], x_to[d])

    def x_next(r, d):
        c = a_half((x + 3 - 2 * d) % 4, r, d)
        return rc(c, c, xs2.at[d, r], xr2.at[d, r], x_to[d])

    def x_last(r, d):
        c = a_half((x + 2) % 4, r, d)
        return rc(c, c, xs2.at[d, r], xr2.at[d, r], x_to[d])

    def e_send(r, d):
        src = zsrc.at[r, pl.ds(d * 64, 64)]
        return rc(src, relay.at[r, d], es.at[d, r], er.at[d, r], z_two[d])

    def f_send(r, d):
        return rc(relay.at[r, d], zdst.at[r, pl.ds(d * 64, 64)], fs.at[d, r], fr.at[d, r], z_two[d])

    def product(r, h):
        rows = pl.ds(pl.multiple_of(r * BLOCK, BLOCK), BLOCK)
        acc = None
        for i in range(4):
            w = jnp.concatenate(
                [wbuf[2 * h + n // 2, n % 2, i] for n in range(4)], axis=1
            )
            part = dot(abuf[i, rows, :], w)
            acc = part if acc is None else acc + part
        return acc

    def step(it, carry):
        @pl.when(it < 4)
        def _():
            attend(it)
            for d in range(2):
                x_send(it, d).start()

        @pl.when(it == 1)
        def _():
            for d in range(2):
                yy = (y + 3 - 2 * d) % 4
                wy(yy, d, wys.at[d], wyr.at[d]).wait_recv()
                wy_half(yy, d).start()
                wc(3 - 2 * d, core).start()

        @pl.when(it == 2)
        def _():
            for d in range(2):
                wy_half((y + 2) % 4, d).wait_recv()
            wc(2, core).start()
            for off in range(4):
                wc(off, 1 - core).wait_recv()

        @pl.when((it >= 1) & (it < 5))
        def _():
            for d in range(2):
                x_got(it - 1, d).wait_recv()
                x_next(it - 1, d).start()

        @pl.when((it >= 2) & (it < 6))
        def _():
            r = it - 2
            for d in range(2):
                x_last(r, d).wait_recv()
            zsrc[r] = product(r, 1 - zh).astype(jnp.bfloat16)
            for d in range(2):
                e_send(r, d).start()
            own[r] = product(r, zh)

        @pl.when((it >= 3) & (it < 7))
        def _():
            for d in range(2):
                e_send(it - 3, d).wait_recv()
                f_send(it - 3, d).start()

        @pl.when(it >= 4)
        def _():
            r = it - 4
            for d in range(2):
                f_send(r, d).wait_recv()
            rows = pl.ds(pl.multiple_of(r * BLOCK, BLOCK), BLOCK)
            out_ref[rows, :] = (own[r] + zdst[r].astype(jnp.float32)).astype(jnp.bfloat16)

        return carry

    lax.fori_loop(0, 8, step, 0)

    for t in range(4):
        @pl.when(p >= t)
        def _(t=t):
            if t < 3:
                @pl.when(p < 3)
                def _():
                    z_send(t).wait_send()
            for d in range(2):
                y_send(t, d).wait_send()
                y_next(t, d).wait_send()
            for off in range(4):
                c_send(t, off).wait_send()

    @pl.when(x != p)
    def _():
        w_move().wait_send()

    for i in range(4):
        @pl.when((p >= x) & (p < 3))
        def _(i=i):
            wz_send(i, 0).wait_send()

        @pl.when((p <= x) & (p > 0))
        def _(i=i):
            wz_send(i, 1).wait_send()

    for d in range(2):
        wy(y, d, wys.at[d], wyr.at[d]).wait_send()
        wy_half((y + 3 - 2 * d) % 4, d).wait_send()
    for off in range(4):
        wc(off, core).wait_send()

    def drain(r, carry):
        for d in range(2):
            x_send(r, d).wait_send()
            x_next(r, d).wait_send()
            e_send(r, d).wait_send()
            f_send(r, d).wait_send()
        return carry

    lax.fori_loop(0, 4, drain, 0)


def shards(queries, key_rows, value_rows, out_weight, vertical, slash_offsets):
    bf16 = jnp.bfloat16
    dma = pltpu.SemaphoreType.DMA
    smem = pl.BlockSpec(memory_space=pltpu.SMEM)
    vmem = pl.BlockSpec(memory_space=pltpu.VMEM)
    anyspace = pl.BlockSpec(memory_space=pl.ANY)
    return pl.pallas_call(
        kernel,
        out_shape=jax.ShapeDtypeStruct((ROWS, ROWS), bf16),
        in_specs=[smem, smem, vmem, anyspace, anyspace, anyspace],
        out_specs=vmem,
        scratch_shapes=[
            pltpu.VMEM((132, 2, BLOCK, HEAD_DIM), bf16),
            pltpu.VMEM((4, 2, 4, ROWS, 128), bf16),
            pltpu.VMEM((4, ROWS, ROWS), bf16),
            pltpu.VMEM((GROUP, PICK, HEAD_DIM), bf16),
            pltpu.VMEM((GROUP, PICK, HEAD_DIM), bf16),
            pltpu.VMEM((GROUP, BLOCK, WIN), jnp.float32),
            pltpu.VMEM((RBLK, BLOCK, ROWS), jnp.float32),
            pltpu.VMEM((RBLK, BLOCK, ROWS), bf16),
            pltpu.VMEM((RBLK, 2, 64, ROWS), bf16),
            pltpu.VMEM((RBLK, BLOCK, ROWS), bf16),
            dma((3,)),
            dma((4,)), dma((4,)),
            dma((2, 4)), dma((2, 4)), dma((2, 4)), dma((2, 4)),
            dma((4, 4)), dma((4, 4)),
            dma((1,)), dma((4,)),
            dma((2, 4)), dma((4,)),
            dma((2,)), dma((2,)), dma((2,)), dma((2,)),
            dma((4,)), dma((4,)),
            dma((2, 4)), dma((2, 4)), dma((2, 4)), dma((2, 4)),
            dma((2, 4)), dma((2, 4)), dma((2, 4)), dma((2, 4)),
        ],
        compiler_params=pltpu.CompilerParams(
            collective_id=0, has_side_effects=True, vmem_limit_bytes=56 * 1024 * 1024
        ),
    )(
        vertical,
        slash_offsets,
        queries,
        key_rows.reshape(4, BLOCK, HEAD_DIM),
        value_rows.reshape(4, BLOCK, HEAD_DIM),
        out_weight,
    )


def solution(mesh):
    in_specs = (P("seq", "kv"), P("seq", "kv"), P("seq", "kv"), P("kv", "seq"), P(), P())
    out_specs = P("seq", "kv")
    return jax.shard_map(shards, mesh=mesh, in_specs=in_specs, out_specs=out_specs, check_vma=False)
```

```python
import functools
import math

import jax
import jax.numpy as jnp
from jax import lax
from jax.experimental import pallas as pl
from jax.experimental.pallas import tpu as pltpu
from jax.sharding import PartitionSpec as P

MESH = pl.DeviceIdType.MESH
HEAD_DIM = 128
BLOCK = 128
GROUP = 4
ROWS = 512
NV = 16
NS = 16
NPICK = NV + 1
RBLK = ROWS // BLOCK
WIN = 5 * BLOCK
PICK = NPICK * BLOCK
NEG = -1e30
SCALE = math.log2(math.e) / math.sqrt(HEAD_DIM)


def dot(a, b):
    return jnp.dot(a, b, preferred_element_type=jnp.float32)


def dot_t(a, b):
    return lax.dot_general(a, b, (((1,), (1,)), ((), ())), preferred_element_type=jnp.float32)


def kernel(
    vert, slash, q_ref, k_hbm, v_hbm, w_hbm, out_ref,
    kvbuf, wbuf, abuf, kcat, vcat, sbias, zsrc, zdst,
    lsem, zs, zr, ys, yr, ys2, yr2, cs, cr,
    wxs, wxr, wzs, wzr, wys, wyr, wys2, wyr2, wcs, wcr,
    xs, xr, xs2, xr2, es, er,
):
    seq = lax.axis_index("seq")
    kv = lax.axis_index("kv")
    core = seq % 2
    y = (seq // 2) % 4
    p = seq // 8
    x = kv // 2
    zh = kv % 2
    z = zh * 4 + p

    def dev(x_, y_, z_, c_):
        return (((z_ % 4) * 4 + y_) * 2 + c_, x_ * 2 + z_ // 4)

    sib = dev(x, y, z, 1 - core)
    y_to = [dev(x, (y + 1) % 4, z, core), dev(x, (y + 3) % 4, z, core)]
    z_up = dev(x, y, (z + 1) % 8, core)
    z_dn = dev(x, y, (z + 7) % 8, core)
    z_far = dev(x, y, (z + 4) % 8, core)
    x_to = [dev((x + 1) % 4, y, z, core), dev((x + 3) % 4, y, z, core)]

    def rc(src, dst, ss, rs, d):
        return pltpu.make_async_remote_copy(
            src_ref=src, dst_ref=dst, send_sem=ss, recv_sem=rs, device_id=d, device_id_type=MESH
        )

    def chunk(q, yy, c):
        return kvbuf.at[pl.ds(4 + 4 * ((q * 4 + yy) * 2 + c), 4)]

    def half(q, yy, c, h):
        return kvbuf.at[pl.ds(4 + 4 * ((q * 4 + yy) * 2 + c) + 2 * h, 2)]

    base = 4 + 4 * seq
    copies = [
        pltpu.make_async_copy(k_hbm, kvbuf.at[pl.ds(base, 4), 0], lsem.at[0]),
        pltpu.make_async_copy(v_hbm, kvbuf.at[pl.ds(base, 4), 1], lsem.at[1]),
    ]
    for c in copies:
        c.start()
    w_local = pltpu.make_async_copy(w_hbm, wbuf.at[x, core, y], lsem.at[2])
    w_stays = (x == p) & (y == x)

    @pl.when(w_stays)
    def _():
        w_local.start()

    barrier = pltpu.get_barrier_semaphore()
    partners = [sib, *y_to, z_up, z_dn, z_far, *x_to]
    for d in partners:
        pl.semaphore_signal(barrier, inc=1, device_id=d, device_id_type=MESH)

    @pl.when(jnp.logical_not(w_stays))
    def _():
        pl.semaphore_signal(barrier, inc=1, device_id=dev(p, x, z, core), device_id_type=MESH)

    for yy in range(4):
        @pl.when((x == p) & ((y != x) | (yy != y)))
        def _(yy=yy):
            pl.semaphore_signal(barrier, inc=1, device_id=dev(y, yy, z, core), device_id_type=MESH)

    for c in copies:
        c.wait()
    holds = jnp.where(x == p, 4, 0) + jnp.where(w_stays, -1, 1)
    pl.semaphore_wait(barrier, len(partners) + holds)

    def z_send(t):
        return rc(chunk(p - t, y, core), chunk(p - t, y, core), zs.at[t], zr.at[t + 1], z_up)

    def y_send(t, d):
        return rc(chunk(p - t, y, core), chunk(p - t, y, core), ys.at[d, t], yr.at[d, t], y_to[d])

    def y_got(t, d):
        c = chunk(p - t, (y + 3 - 2 * d) % 4, core)
        return rc(c, c, ys.at[d, t], yr.at[d, t], y_to[d])

    def y_next(t, d):
        c = half(p - t, (y + 3 - 2 * d) % 4, core, d)
        return rc(c, c, ys2.at[d, t], yr2.at[d, t], y_to[d])

    def y_far(t, d):
        c = half(p - t, (y + 2) % 4, core, d)
        return rc(c, c, ys2.at[d, t], yr2.at[d, t], y_to[d])

    def c_send(t, off):
        c = chunk(p - t, (y + off) % 4, core)
        return rc(c, c, cs.at[t, off], cr.at[t, off], sib)

    def c_got(t, off):
        c = chunk(p - t, (y + off) % 4, 1 - core)
        return rc(c, c, cs.at[t, off], cr.at[t, off], sib)

    def enter(t):
        @pl.when(p >= t)
        def _():
            if t > 0:
                c = chunk(p - t, y, core)
                rc(c, c, zs.at[t], zr.at[t], z_up).wait_recv()
            if t < 3:
                @pl.when(p < 3)
                def _():
                    z_send(t).start()
            for d in range(2):
                y_send(t, d).start()
            c_send(t, 0).start()

    def onward(t):
        @pl.when(p >= t)
        def _():
            for d in range(2):
                y_got(t, d).wait_recv()
                y_next(t, d).start()
                c_send(t, 3 - 2 * d).start()

    def finish(t):
        @pl.when(p >= t)
        def _():
            for d in range(2):
                y_far(t, d).wait_recv()
            c_send(t, 2).start()

    def w_move():
        return rc(w_hbm, wbuf.at[x, core, y], wxs.at[0], wxr.at[y], dev(p, x, z, core))

    def w_order(i):
        return (i + 2 * (1 - zh)) % 4

    def wz_send(i, d):
        c = wbuf.at[y, core, w_order(i)]
        return rc(c, c, wzs.at[d, i], wzr.at[i], z_up if d == 0 else z_dn)

    def w_pass(i):
        c = wbuf.at[y, core, w_order(i)]

        @pl.when((x == p) & (y == x) & (w_order(i) == y))
        def _():
            w_local.wait()

        @pl.when((x == p) & ((y != x) | (w_order(i) != y)))
        def _():
            rc(c, c, wxs.at[0], wxr.at[w_order(i)], sib).wait_recv()

        @pl.when(x != p)
        def _():
            rc(c, c, wzs.at[0, i], wzr.at[i], sib).wait_recv()

        @pl.when((p >= x) & (p < 3))
        def _():
            wz_send(i, 0).start()

        @pl.when((p <= x) & (p > 0))
        def _():
            wz_send(i, 1).start()

    def w_half(yy, c_, k):
        return wbuf.at[yy, c_, pl.ds(2 * ((1 - zh + k) % 2), 2)]

    def wy_send(k, d):
        c = w_half(y, core, k)
        return rc(c, c, wys.at[d, k], wyr.at[d, k], y_to[d])

    def wy_got(k, d):
        c = w_half((y + 3 - 2 * d) % 4, core, k)
        return rc(c, c, wys.at[d, k], wyr.at[d, k], y_to[d])

    def wy_next(k, d):
        c = wbuf.at[(y + 3 - 2 * d) % 4, core, 2 * ((1 - zh + k) % 2) + d]
        return rc(c, c, wys2.at[d, k], wyr2.at[d, k], y_to[d])

    def wy_far(k, d):
        c = wbuf.at[(y + 2) % 4, core, 2 * ((1 - zh + k) % 2) + d]
        return rc(c, c, wys2.at[d, k], wyr2.at[d, k], y_to[d])

    def wc(k, off, c_):
        c = w_half((y + off) % 4, c_, k)
        return rc(c, c, wcs.at[k, off], wcr.at[k, off], sib)

    def w_enter(k):
        for d in range(2):
            wy_send(k, d).start()
        wc(k, 0, core).start()

    def w_onward(k):
        for d in range(2):
            wy_got(k, d).wait_recv()
            wy_next(k, d).start()
            wc(k, 3 - 2 * d, core).start()

    def w_finish(k):
        for d in range(2):
            wy_far(k, d).wait_recv()
        wc(k, 2, core).start()

    def w_done(k):
        for off in range(4):
            wc(k, off, 1 - core).wait_recv()

    @pl.when(jnp.logical_not(w_stays))
    def _():
        w_move().start()

    enter(0)

    kvbuf[0:4] = jnp.zeros((4, 2, BLOCK, HEAD_DIM), jnp.bfloat16)

    def mask_step(n, carry):
        m, strip = n // 4, n % 4
        i = lax.broadcasted_iota(jnp.int32, (32, WIN), 0) + strip * 32
        j = lax.broadcasted_iota(jnp.int32, (32, WIN), 1)
        d = 4 * BLOCK + i - j
        b = jnp.where(d == 0, 0.0, NEG)
        for e in range(NS):
            b = jnp.where(d == slash[e, kv * GROUP + m] + 1, 0.0, b)
        sbias[m, pl.ds(pl.multiple_of(strip * 32, 32), 32), :] = b
        return carry

    lax.fori_loop(0, 16, mask_step, 0)

    enter(1)
    onward(0)
    enter(2)
    w_pass(0)
    onward(1)
    finish(0)
    w_pass(1)
    enter(3)
    w_pass(2)
    w_pass(3)
    onward(2)
    finish(1)
    onward(3)
    w_enter(0)
    finish(2)
    finish(3)
    w_enter(1)
    for t in range(4):
        @pl.when(p >= t)
        def _(t=t):
            for off in range(4):
                c_got(t, off).wait_recv()

    def gather(m, carry):
        for j in range(NPICK):
            b = 0 if j == 0 else vert[j - 1, kv * GROUP + m] + 1
            at = 4 + (0 if j == 0 else jnp.where(b < 4 * seq + 4, b, 0))
            kcat[m, j * BLOCK : (j + 1) * BLOCK, :] = kvbuf[at, 0]
            vcat[m, j * BLOCK : (j + 1) * BLOCK, :] = kvbuf[at, 1]
        return carry

    lax.fori_loop(0, GROUP, gather, 0)

    wi = lax.broadcasted_iota(jnp.int32, (BLOCK, WIN), 0)
    wj = lax.broadcasted_iota(jnp.int32, (BLOCK, WIN), 1)
    lane = lax.broadcasted_iota(jnp.int32, (1, WIN), 1)

    def attend(r):
        rows = pl.ds(pl.multiple_of(r * BLOCK, BLOCK), BLOCK)
        here = 4 * seq + r
        for m in range(GROUP):
            cols = slice(m * HEAD_DIM, (m + 1) * HEAD_DIM)
            q = q_ref[rows, cols]
            kw = kvbuf[pl.ds(here, 5), 0].reshape(WIN, HEAD_DIM)
            vw = kvbuf[pl.ds(here, 5), 1].reshape(WIN, HEAD_DIM)
            bcol = here - 4 + lane // BLOCK
            oncol = bcol <= 0
            pb = [jnp.full((1, BLOCK), jnp.where(here > 0, 0.0, NEG), jnp.float32)]
            for e in range(NV):
                b = vert[e, kv * GROUP + m] + 1
                oncol = oncol | (bcol == b)
                pb.append(jnp.full((1, BLOCK), jnp.where(b < here, 0.0, NEG), jnp.float32))
            alt = jnp.where((wj >= 4 * BLOCK) & (wi >= wj - 4 * BLOCK), 0.0, NEG)
            bias = jnp.where(oncol, alt, sbias[m])
            sw = dot_t(q, kw) + bias
            sp = dot_t(q, kcat[m]) + jnp.concatenate(pb, axis=1)
            peak = jnp.maximum(
                jnp.max(sw, axis=1, keepdims=True), jnp.max(sp, axis=1, keepdims=True)
            )
            pw = jnp.exp2((sw - peak) * SCALE).astype(jnp.bfloat16)
            pp = jnp.exp2((sp - peak) * SCALE).astype(jnp.bfloat16)
            ones_w = jnp.ones((WIN, HEAD_DIM), jnp.bfloat16)
            ones_p = jnp.ones((PICK, HEAD_DIM), jnp.bfloat16)
            o = dot(pw, jnp.concatenate([vw, ones_w], axis=1))
            o = o + dot(pp, jnp.concatenate([vcat[m], ones_p], axis=1))
            abuf[x, rows, cols] = (o[:, :HEAD_DIM] / o[:, HEAD_DIM:]).astype(jnp.bfloat16)

    def a_part(xx, r):
        return abuf.at[xx, pl.ds(pl.multiple_of(r * BLOCK, BLOCK), BLOCK)]

    def a_half(xx, r, d):
        return abuf.at[xx, pl.ds(pl.multiple_of(r * BLOCK + d * 64, 64), 64)]

    def x_send(r, d):
        return rc(a_part(x, r), a_part(x, r), xs.at[d, r], xr.at[d, r], x_to[d])

    def x_got(r, d):
        c = a_part((x + 3 - 2 * d) % 4, r)
        return rc(c, c, xs.at[d, r], xr.at[d, r], x_to[d])

    def x_next(r, d):
        c = a_half((x + 3 - 2 * d) % 4, r, d)
        return rc(c, c, xs2.at[d, r], xr2.at[d, r], x_to[d])

    def x_last(r, d):
        c = a_half((x + 2) % 4, r, d)
        return rc(c, c, xs2.at[d, r], xr2.at[d, r], x_to[d])

    def e_send(r, d):
        c = pl.ds(d * 64, 64)
        return rc(zsrc.at[r, c], zdst.at[r, c], es.at[d, r], er.at[d, r], z_far)

    def product(r, h):
        rows = pl.ds(pl.multiple_of(r * BLOCK, BLOCK), BLOCK)
        acc = None
        for i in range(4):
            w = jnp.concatenate(
                [wbuf[i, n % 2, 2 * h + n // 2] for n in range(4)], axis=1
            )
            part = dot(abuf[i, rows, :], w)
            acc = part if acc is None else acc + part
        return acc

    def step(it, carry):
        @pl.when(it < 4)
        def _():
            attend(it)
            for d in range(2):
                x_send(it, d).start()

        @pl.when(it == 1)
        def _():
            w_onward(0)

        @pl.when(it == 2)
        def _():
            w_finish(0)
            w_done(0)
            w_onward(1)

        @pl.when(it == 3)
        def _():
            w_finish(1)

        @pl.when(it == 4)
        def _():
            w_done(1)

        @pl.when((it >= 1) & (it < 5))
        def _():
            for d in range(2):
                x_got(it - 1, d).wait_recv()
                x_next(it - 1, d).start()

        @pl.when((it >= 2) & (it < 6))
        def _():
            r = it - 2
            for d in range(2):
                x_last(r, d).wait_recv()
            zsrc[r] = product(r, 1 - zh).astype(jnp.bfloat16)
            for d in range(2):
                e_send(r, d).start()

        @pl.when(it >= 4)
        def _():
            r = it - 4
            own = product(r, zh)
            for d in range(2):
                e_send(r, d).wait_recv()
            rows = pl.ds(pl.multiple_of(r * BLOCK, BLOCK), BLOCK)
            out_ref[rows, :] = (own + zdst[r].astype(jnp.float32)).astype(jnp.bfloat16)

        return carry

    lax.fori_loop(0, 8, step, 0)

    for t in range(4):
        @pl.when(p >= t)
        def _(t=t):
            if t < 3:
                @pl.when(p < 3)
                def _():
                    z_send(t).wait_send()
            for d in range(2):
                y_send(t, d).wait_send()
                y_next(t, d).wait_send()
            for off in range(4):
                c_send(t, off).wait_send()

    @pl.when(jnp.logical_not(w_stays))
    def _():
        w_move().wait_send()

    for i in range(4):
        @pl.when((p >= x) & (p < 3))
        def _(i=i):
            wz_send(i, 0).wait_send()

        @pl.when((p <= x) & (p > 0))
        def _(i=i):
            wz_send(i, 1).wait_send()

    for k in range(2):
        for d in range(2):
            wy_send(k, d).wait_send()
            wy_next(k, d).wait_send()
        for off in range(4):
            wc(k, off, core).wait_send()

    def drain(r, carry):
        for d in range(2):
            x_send(r, d).wait_send()
            x_next(r, d).wait_send()
            e_send(r, d).wait_send()
        return carry

    lax.fori_loop(0, 4, drain, 0)


def shards(queries, key_rows, value_rows, out_weight, vertical, slash_offsets):
    bf16 = jnp.bfloat16
    dma = pltpu.SemaphoreType.DMA
    smem = pl.BlockSpec(memory_space=pltpu.SMEM)
    vmem = pl.BlockSpec(memory_space=pltpu.VMEM)
    anyspace = pl.BlockSpec(memory_space=pl.ANY)
    return pl.pallas_call(
        kernel,
        out_shape=jax.ShapeDtypeStruct((ROWS, ROWS), bf16),
        in_specs=[smem, smem, vmem, anyspace, anyspace, anyspace],
        out_specs=vmem,
        scratch_shapes=[
            pltpu.VMEM((132, 2, BLOCK, HEAD_DIM), bf16),
            pltpu.VMEM((4, 2, 4, ROWS, 128), bf16),
            pltpu.VMEM((4, ROWS, ROWS), bf16),
            pltpu.VMEM((GROUP, PICK, HEAD_DIM), bf16),
            pltpu.VMEM((GROUP, PICK, HEAD_DIM), bf16),
            pltpu.VMEM((GROUP, BLOCK, WIN), jnp.float32),
            pltpu.VMEM((RBLK, BLOCK, ROWS), bf16),
            pltpu.VMEM((RBLK, BLOCK, ROWS), bf16),
            dma((3,)),
            dma((4,)), dma((4,)),
            dma((2, 4)), dma((2, 4)), dma((2, 4)), dma((2, 4)),
            dma((4, 4)), dma((4, 4)),
            dma((1,)), dma((4,)),
            dma((2, 4)), dma((4,)),
            dma((2, 2)), dma((2, 2)), dma((2, 2)), dma((2, 2)),
            dma((2, 4)), dma((2, 4)),
            dma((2, 4)), dma((2, 4)), dma((2, 4)), dma((2, 4)),
            dma((2, 4)), dma((2, 4)),
        ],
        compiler_params=pltpu.CompilerParams(
            collective_id=0, has_side_effects=True, vmem_limit_bytes=56 * 1024 * 1024
        ),
    )(
        vertical.T,
        slash_offsets.T,
        queries,
        key_rows.reshape(4, BLOCK, HEAD_DIM),
        value_rows.reshape(4, BLOCK, HEAD_DIM),
        out_weight,
    )


def solution(mesh):
    in_specs = (P("seq", "kv"), P("seq", "kv"), P("seq", "kv"), P("kv", "seq"), P(), P())
    out_specs = P("seq", "kv")
    return jax.shard_map(shards, mesh=mesh, in_specs=in_specs, out_specs=out_specs, check_vma=False)
```

```python
import functools
import math

import jax
import jax.numpy as jnp
from jax import lax
from jax.experimental import pallas as pl
from jax.experimental.pallas import tpu as pltpu
from jax.sharding import PartitionSpec as P

MESH = pl.DeviceIdType.MESH
HEAD_DIM = 128
BLOCK = 128
GROUP = 4
ROWS = 512
NV = 16
NS = 16
NPICK = NV + 1
RBLK = ROWS // BLOCK
WIN = 5 * BLOCK
PICK = NPICK * BLOCK
NEG = -1e30
UNIT = 2
LAG1 = 1
LAG2 = 2
LAG3 = 4
W_STEPS = [(1, 0, 0), (2, 1, 0), (2, 2, 0), (2, 0, 1), (3, 1, 1), (4, 2, 1)]
SCALE = math.log2(math.e) / math.sqrt(HEAD_DIM)


def dot(a, b):
    return jnp.dot(a, b, preferred_element_type=jnp.float32)


def dot_t(a, b):
    return lax.dot_general(a, b, (((1,), (1,)), ((), ())), preferred_element_type=jnp.float32)


def kernel(
    vert, slash, q_ref, k_hbm, v_hbm, w_hbm, out_ref,
    kvbuf, wbuf, abuf, sbias, zsrc, zdst,
    lsem, zs, zr, ys, yr, ys2, yr2, cs, cr,
    wxs, wxr, wzs, wzr, wys, wyr, wys2, wyr2, wcs, wcr,
    xs, xr, xs2, xr2, es, er,
):
    seq = lax.axis_index("seq")
    kv = lax.axis_index("kv")
    core = seq % 2
    y = (seq // 2) % 4
    p = seq // 8
    x = kv // 2
    zh = kv % 2
    z = zh * 4 + p

    def dev(x_, y_, z_, c_):
        return (((z_ % 4) * 4 + y_) * 2 + c_, x_ * 2 + z_ // 4)

    sib = dev(x, y, z, 1 - core)
    y_to = [dev(x, (y + 1) % 4, z, core), dev(x, (y + 3) % 4, z, core)]
    z_up = dev(x, y, (z + 1) % 8, core)
    z_dn = dev(x, y, (z + 7) % 8, core)
    z_far = dev(x, y, (z + 4) % 8, core)
    x_to = [dev((x + 1) % 4, y, z, core), dev((x + 3) % 4, y, z, core)]

    def rc(src, dst, ss, rs, d):
        return pltpu.make_async_remote_copy(
            src_ref=src, dst_ref=dst, send_sem=ss, recv_sem=rs, device_id=d, device_id_type=MESH
        )

    def chunk(q, yy, c):
        return kvbuf.at[pl.ds(4 + 4 * ((q * 4 + yy) * 2 + c), 4)]

    def half(q, yy, c, h):
        return kvbuf.at[pl.ds(4 + 4 * ((q * 4 + yy) * 2 + c) + 2 * h, 2)]

    base = 4 + 4 * seq
    copies = [
        pltpu.make_async_copy(k_hbm, kvbuf.at[pl.ds(base, 4), 0], lsem.at[0]),
        pltpu.make_async_copy(v_hbm, kvbuf.at[pl.ds(base, 4), 1], lsem.at[1]),
    ]
    for c in copies:
        c.start()
    w_local = pltpu.make_async_copy(w_hbm, wbuf.at[x, core, y], lsem.at[2])
    w_stays = (x == p) & (y == x)

    @pl.when(w_stays)
    def _():
        w_local.start()

    barrier = pltpu.get_barrier_semaphore()
    partners = [sib, *y_to, z_up, z_dn, z_far, *x_to]
    for d in partners:
        pl.semaphore_signal(barrier, inc=1, device_id=d, device_id_type=MESH)

    @pl.when(jnp.logical_not(w_stays))
    def _():
        pl.semaphore_signal(barrier, inc=1, device_id=dev(p, x, z, core), device_id_type=MESH)

    for yy in range(4):
        @pl.when((x == p) & ((y != x) | (yy != y)))
        def _(yy=yy):
            pl.semaphore_signal(barrier, inc=1, device_id=dev(y, yy, z, core), device_id_type=MESH)

    for c in copies:
        c.wait()
    holds = jnp.where(x == p, 4, 0) + jnp.where(w_stays, -1, 1)
    pl.semaphore_wait(barrier, len(partners) + holds)

    def z_send(t):
        return rc(chunk(p - t, y, core), chunk(p - t, y, core), zs.at[t], zr.at[t + 1], z_up)

    def y_send(t, d):
        return rc(chunk(p - t, y, core), chunk(p - t, y, core), ys.at[d, t], yr.at[d, t], y_to[d])

    def y_got(t, d):
        c = chunk(p - t, (y + 3 - 2 * d) % 4, core)
        return rc(c, c, ys.at[d, t], yr.at[d, t], y_to[d])

    def y_next(t, d):
        c = half(p - t, (y + 3 - 2 * d) % 4, core, d)
        return rc(c, c, ys2.at[d, t], yr2.at[d, t], y_to[d])

    def y_far(t, d):
        c = half(p - t, (y + 2) % 4, core, d)
        return rc(c, c, ys2.at[d, t], yr2.at[d, t], y_to[d])

    def c_send(t, off):
        c = chunk(p - t, (y + off) % 4, core)
        return rc(c, c, cs.at[t, off], cr.at[t, off], sib)

    def c_got(t, off):
        c = chunk(p - t, (y + off) % 4, 1 - core)
        return rc(c, c, cs.at[t, off], cr.at[t, off], sib)

    def enter(t):
        @pl.when(p >= t)
        def _():
            if t > 0:
                c = chunk(p - t, y, core)
                rc(c, c, zs.at[t], zr.at[t], z_up).wait_recv()
            if t < 3:
                @pl.when(p < 3)
                def _():
                    z_send(t).start()
            for d in range(2):
                y_send(t, d).start()
            c_send(t, 0).start()

    def onward(t):
        @pl.when(p >= t)
        def _():
            for d in range(2):
                y_got(t, d).wait_recv()
                y_next(t, d).start()
                c_send(t, 3 - 2 * d).start()

    def finish(t):
        @pl.when(p >= t)
        def _():
            for d in range(2):
                y_far(t, d).wait_recv()
            c_send(t, 2).start()

    def w_move():
        return rc(w_hbm, wbuf.at[x, core, y], wxs.at[0], wxr.at[y], dev(p, x, z, core))

    def w_order(i):
        return (i + 2 * (1 - zh)) % 4

    def wz_send(i, d):
        c = wbuf.at[y, core, w_order(i)]
        return rc(c, c, wzs.at[d, i], wzr.at[i], z_up if d == 0 else z_dn)

    def w_pass(i):
        c = wbuf.at[y, core, w_order(i)]

        @pl.when((x == p) & (y == x) & (w_order(i) == y))
        def _():
            w_local.wait()

        @pl.when((x == p) & ((y != x) | (w_order(i) != y)))
        def _():
            rc(c, c, wxs.at[0], wxr.at[w_order(i)], sib).wait_recv()

        @pl.when(x != p)
        def _():
            rc(c, c, wzs.at[0, i], wzr.at[i], sib).wait_recv()

        @pl.when((p >= x) & (p < 3))
        def _():
            wz_send(i, 0).start()

        @pl.when((p <= x) & (p > 0))
        def _():
            wz_send(i, 1).start()

    def w_pass_all():
        for i in range(4):
            w_pass(i)

    def w_take(i):
        c = wbuf.at[y, core, w_order(i)]
        rc(c, c, wzs.at[0, i], wzr.at[i], sib).wait_recv()

    def w_half(yy, c_, k):
        return wbuf.at[yy, c_, pl.ds(2 * ((1 - zh + k) % 2), 2)]

    def wy_send(k, d):
        c = w_half(y, core, k)
        return rc(c, c, wys.at[d, k], wyr.at[d, k], y_to[d])

    def wy_got(k, d):
        c = w_half((y + 3 - 2 * d) % 4, core, k)
        return rc(c, c, wys.at[d, k], wyr.at[d, k], y_to[d])

    def wy_next(k, d):
        c = wbuf.at[(y + 3 - 2 * d) % 4, core, 2 * ((1 - zh + k) % 2) + d]
        return rc(c, c, wys2.at[d, k], wyr2.at[d, k], y_to[d])

    def wy_far(k, d):
        c = wbuf.at[(y + 2) % 4, core, 2 * ((1 - zh + k) % 2) + d]
        return rc(c, c, wys2.at[d, k], wyr2.at[d, k], y_to[d])

    def wc(k, off, c_):
        c = w_half((y + off) % 4, c_, k)
        return rc(c, c, wcs.at[k, off], wcr.at[k, off], sib)

    def w_enter(k):
        for d in range(2):
            wy_send(k, d).start()
        wc(k, 0, core).start()

    def w_onward(k):
        for d in range(2):
            wy_got(k, d).wait_recv()
            wy_next(k, d).start()
            wc(k, 3 - 2 * d, core).start()

    def w_finish(k):
        for d in range(2):
            wy_far(k, d).wait_recv()
        wc(k, 2, core).start()

    def w_done(k):
        for off in range(4):
            wc(k, off, 1 - core).wait_recv()

    @pl.when(jnp.logical_not(w_stays))
    def _():
        w_move().start()

    enter(0)

    kvbuf[0:4] = jnp.zeros((4, 2, BLOCK, HEAD_DIM), jnp.bfloat16)

    def mask_step(n, carry):
        m, strip = n // 4, n % 4
        i = lax.broadcasted_iota(jnp.int32, (32, WIN), 0) + strip * 32
        j = lax.broadcasted_iota(jnp.int32, (32, WIN), 1)
        d = 4 * BLOCK + i - j
        b = jnp.where(d == 0, 0.0, NEG)
        for e in range(NS):
            b = jnp.where(d == slash[e, kv * GROUP + m] + 1, 0.0, b)
        sbias[m, pl.ds(pl.multiple_of(strip * 32, 32), 32), :] = b
        return carry

    lax.fori_loop(0, 16, mask_step, 0)

    @pl.when((p == 0) | ((p == 3) & (x == 3)))
    def _():
        w_pass_all()

    enter(1)

    @pl.when(p == 1)
    def _():
        w_pass_all()

    onward(0)
    enter(2)

    @pl.when(p == 2)
    def _():
        w_pass_all()

    onward(1)
    finish(0)
    enter(3)
    onward(2)
    finish(1)
    onward(3)

    @pl.when((p == 3) & (x < 3))
    def _():
        w_take(0)
        w_take(1)

    w_enter(0)
    finish(2)
    finish(3)

    @pl.when((p == 3) & (x < 3))
    def _():
        w_take(2)
        w_take(3)

    w_enter(1)
    for t in range(4):
        @pl.when(p >= t)
        def _(t=t):
            for off in range(4):
                c_got(t, off).wait_recv()

    wi = lax.broadcasted_iota(jnp.int32, (BLOCK, WIN), 0)
    wj = lax.broadcasted_iota(jnp.int32, (BLOCK, WIN), 1)
    lane = lax.broadcasted_iota(jnp.int32, (1, WIN), 1)

    def attend(r):
        rows = pl.ds(pl.multiple_of(r * BLOCK, BLOCK), BLOCK)
        here = 4 * seq + r
        kw = kvbuf[pl.ds(here, 5), 0].reshape(WIN, HEAD_DIM)
        vw = kvbuf[pl.ds(here, 5), 1].reshape(WIN, HEAD_DIM)
        vw = jnp.concatenate([vw, jnp.ones((WIN, HEAD_DIM), jnp.bfloat16)], axis=1)
        ones = jnp.ones((PICK, HEAD_DIM), jnp.bfloat16)
        bcol = here - 4 + lane // BLOCK
        alt = jnp.where((wj >= 4 * BLOCK) & (wi >= wj - 4 * BLOCK), 0.0, NEG)
        for m in range(GROUP):
            q = q_ref[rows, m * HEAD_DIM : (m + 1) * HEAD_DIM]
            oncol = bcol <= 0
            pb = [jnp.full((1, BLOCK), jnp.where(here > 0, 0.0, NEG), jnp.float32)]
            at = [4]
            for e in range(NV):
                b = vert[e, kv * GROUP + m] + 1
                oncol = oncol | (bcol == b)
                pb.append(jnp.full((1, BLOCK), jnp.where(b < here, 0.0, NEG), jnp.float32))
                at.append(4 + jnp.where(b < here, b, 0))
            kp = jnp.concatenate([kvbuf[a, 0] for a in at], axis=0)
            vp = jnp.concatenate([kvbuf[a, 1] for a in at], axis=0)
            sw = dot_t(q, kw) + jnp.where(oncol, alt, sbias[m])
            sp = dot_t(q, kp) + jnp.concatenate(pb, axis=1)
            peak = jnp.maximum(
                jnp.max(sw, axis=1, keepdims=True), jnp.max(sp, axis=1, keepdims=True)
            )
            pw = jnp.exp2((sw - peak) * SCALE).astype(jnp.bfloat16)
            pp = jnp.exp2((sp - peak) * SCALE).astype(jnp.bfloat16)
            o = dot(pw, vw) + dot(pp, jnp.concatenate([vp, ones], axis=1))
            abuf[x, r, m] = (o[:, :HEAD_DIM] / o[:, HEAD_DIM:]).astype(jnp.bfloat16)

    def a_part(xx, r, m):
        return abuf.at[xx, r, pl.ds(m - UNIT + 1, UNIT)]

    def a_half(xx, r, m, d):
        if UNIT > 1:
            return abuf.at[xx, r, pl.ds(m - UNIT + 1 + d * (UNIT // 2), UNIT // 2)]
        return abuf.at[xx, r, m, pl.ds(d * 64, 64)]

    def x_copy(c, ss, rs, r, m, d):
        n = r * GROUP + m
        return rc(c, c, ss.at[d, n], rs.at[d, n], x_to[d])

    def x_send(r, m, d):
        return x_copy(a_part(x, r, m), xs, xr, r, m, d)

    def x_got(r, m, d):
        return x_copy(a_part((x + 3 - 2 * d) % 4, r, m), xs, xr, r, m, d)

    def x_next(r, m, d):
        return x_copy(a_half((x + 3 - 2 * d) % 4, r, m, d), xs2, xr2, r, m, d)

    def x_last(r, m, d):
        return x_copy(a_half((x + 2) % 4, r, m, d), xs2, xr2, r, m, d)

    def e_send(r, d):
        c = pl.ds(d * 64, 64)
        return rc(zsrc.at[r, c], zdst.at[r, c], es.at[d, r], er.at[d, r], z_far)

    def product(r, h):
        acc = None
        for i in range(4):
            w = jnp.concatenate(
                [wbuf[i, n % 2, 2 * h + n // 2] for n in range(4)], axis=1
            )
            a = jnp.concatenate([abuf[i, r, m] for m in range(GROUP)], axis=1)
            part = dot(a, w)
            acc = part if acc is None else acc + part
        return acc

    ends = range(UNIT - 1, GROUP, UNIT)

    def step(it, carry):
        @pl.when(it < RBLK)
        def _():
            attend(it)
            for m in ends:
                for d in range(2):
                    x_send(it, m, d).start()

        for at, act, k in W_STEPS:
            @pl.when(it == at)
            def _(act=act, k=k):
                (w_onward, w_finish, w_done)[act](k)

        @pl.when((it >= LAG1) & (it < RBLK + LAG1))
        def _():
            for m in ends:
                for d in range(2):
                    x_got(it - LAG1, m, d).wait_recv()
                    x_next(it - LAG1, m, d).start()

        @pl.when((it >= LAG2) & (it < RBLK + LAG2))
        def _():
            r = it - LAG2
            for m in ends:
                for d in range(2):
                    x_last(r, m, d).wait_recv()
            zsrc[r] = product(r, 1 - zh).astype(jnp.bfloat16)
            for d in range(2):
                e_send(r, d).start()

        @pl.when(it >= LAG3)
        def _():
            r = it - LAG3
            mine = product(r, zh)
            for d in range(2):
                e_send(r, d).wait_recv()
            rows = pl.ds(pl.multiple_of(r * BLOCK, BLOCK), BLOCK)
            out_ref[rows, :] = (mine + zdst[r].astype(jnp.float32)).astype(jnp.bfloat16)

        return carry

    lax.fori_loop(0, RBLK + LAG3, step, 0)

    for t in range(4):
        @pl.when(p >= t)
        def _(t=t):
            if t < 3:
                @pl.when(p < 3)
                def _():
                    z_send(t).wait_send()
            for d in range(2):
                y_send(t, d).wait_send()
                y_next(t, d).wait_send()
            for off in range(4):
                c_send(t, off).wait_send()

    @pl.when(jnp.logical_not(w_stays))
    def _():
        w_move().wait_send()

    for i in range(4):
        @pl.when((p >= x) & (p < 3))
        def _(i=i):
            wz_send(i, 0).wait_send()

        @pl.when((p <= x) & (p > 0))
        def _(i=i):
            wz_send(i, 1).wait_send()

    for k in range(2):
        for d in range(2):
            wy_send(k, d).wait_send()
            wy_next(k, d).wait_send()
        for off in range(4):
            wc(k, off, core).wait_send()

    def drain(r, carry):
        for d in range(2):
            for m in range(UNIT - 1, GROUP, UNIT):
                x_send(r, m, d).wait_send()
                x_next(r, m, d).wait_send()
            e_send(r, d).wait_send()
        return carry

    lax.fori_loop(0, 4, drain, 0)


def shards(queries, key_rows, value_rows, out_weight, vertical, slash_offsets):
    bf16 = jnp.bfloat16
    dma = pltpu.SemaphoreType.DMA
    smem = pl.BlockSpec(memory_space=pltpu.SMEM)
    vmem = pl.BlockSpec(memory_space=pltpu.VMEM)
    anyspace = pl.BlockSpec(memory_space=pl.ANY)
    return pl.pallas_call(
        kernel,
        out_shape=jax.ShapeDtypeStruct((ROWS, ROWS), bf16),
        in_specs=[smem, smem, vmem, anyspace, anyspace, anyspace],
        out_specs=vmem,
        scratch_shapes=[
            pltpu.VMEM((132, 2, BLOCK, HEAD_DIM), bf16),
            pltpu.VMEM((4, 2, 4, ROWS, 128), bf16),
            pltpu.VMEM((4, RBLK, GROUP, BLOCK, HEAD_DIM), bf16),
            pltpu.VMEM((GROUP, BLOCK, WIN), jnp.float32),
            pltpu.VMEM((RBLK, BLOCK, ROWS), bf16),
            pltpu.VMEM((RBLK, BLOCK, ROWS), bf16),
            dma((3,)),
            dma((4,)), dma((4,)),
            dma((2, 4)), dma((2, 4)), dma((2, 4)), dma((2, 4)),
            dma((4, 4)), dma((4, 4)),
            dma((1,)), dma((4,)),
            dma((2, 4)), dma((4,)),
            dma((2, 2)), dma((2, 2)), dma((2, 2)), dma((2, 2)),
            dma((2, 4)), dma((2, 4)),
            dma((2, 16)), dma((2, 16)), dma((2, 16)), dma((2, 16)),
            dma((2, 4)), dma((2, 4)),
        ],
        compiler_params=pltpu.CompilerParams(
            collective_id=0, has_side_effects=True, vmem_limit_bytes=56 * 1024 * 1024
        ),
    )(
        vertical.T,
        slash_offsets.T,
        queries,
        key_rows.reshape(4, BLOCK, HEAD_DIM),
        value_rows.reshape(4, BLOCK, HEAD_DIM),
        out_weight,
    )


def solution(mesh):
    in_specs = (P("seq", "kv"), P("seq", "kv"), P("seq", "kv"), P("kv", "seq"), P(), P())
    out_specs = P("seq", "kv")
    return jax.shard_map(shards, mesh=mesh, in_specs=in_specs, out_specs=out_specs, check_vma=False)
```

```python
import functools
import math

import jax
import jax.numpy as jnp
from jax import lax
from jax.experimental import pallas as pl
from jax.experimental.pallas import tpu as pltpu
from jax.sharding import PartitionSpec as P

MESH = pl.DeviceIdType.MESH
HEAD_DIM = 128
BLOCK = 128
GROUP = 4
ROWS = 512
NV = 16
NS = 16
NPICK = NV + 1
RBLK = ROWS // BLOCK
WIN = 5 * BLOCK
PICK = NPICK * BLOCK
NEG = -1e30
UNIT = 2
LAG2 = 2
LAG3 = 6
LATE = 0
W_STEPS = [(1, 0, 0), (2, 1, 0), (2, 2, 0)]
W_LATER = [(3, 0, 1), (4, 1, 1), (5, 2, 1)]
SCALE = math.log2(math.e) / math.sqrt(HEAD_DIM)


def dot(a, b):
    return jnp.dot(a, b, preferred_element_type=jnp.float32)


def dot_t(a, b):
    return lax.dot_general(a, b, (((1,), (1,)), ((), ())), preferred_element_type=jnp.float32)


def kernel(
    vert, slash, q_ref, k_hbm, v_hbm, w_hbm, out_ref,
    kvbuf, wbuf, abuf, sbias, zsrc, zdst,
    lsem, zs, zr, zfs, zfr, ys, yr, ys2, yr2, cs, cr,
    wxs, wxr, wzs, wzr, wys, wyr, wys2, wyr2, wcs, wcr,
    xs, xr, xs2, xr2, es, er,
):
    seq = lax.axis_index("seq")
    kv = lax.axis_index("kv")
    core = seq % 2
    y = (seq // 2) % 4
    p = seq // 8
    x = kv // 2
    zh = kv % 2
    z = zh * 4 + p

    def dev(x_, y_, z_, c_):
        return (((z_ % 4) * 4 + y_) * 2 + c_, x_ * 2 + z_ // 4)

    sib = dev(x, y, z, 1 - core)
    y_to = [dev(x, (y + 1) % 4, z, core), dev(x, (y + 3) % 4, z, core)]
    x_two = dev((x + 2) % 4, y, z, core)
    y_two = dev(x, (y + 2) % 4, z, core)
    z_up = dev(x, y, (z + 1) % 8, core)
    z_dn = dev(x, y, (z + 7) % 8, core)
    z_far = dev(x, y, (z + 4) % 8, core)
    x_to = [dev((x + 1) % 4, y, z, core), dev((x + 3) % 4, y, z, core)]

    def rc(src, dst, ss, rs, d):
        return pltpu.make_async_remote_copy(
            src_ref=src, dst_ref=dst, send_sem=ss, recv_sem=rs, device_id=d, device_id_type=MESH
        )

    def chunk(q, yy, c):
        return kvbuf.at[pl.ds(4 + 4 * ((q * 4 + yy) * 2 + c), 4)]

    def half(q, yy, c, h):
        return kvbuf.at[pl.ds(4 + 4 * ((q * 4 + yy) * 2 + c) + 2 * h, 2)]

    base = 4 + 4 * seq
    copies = [
        pltpu.make_async_copy(k_hbm, kvbuf.at[pl.ds(base, 4), 0], lsem.at[0]),
        pltpu.make_async_copy(v_hbm, kvbuf.at[pl.ds(base, 4), 1], lsem.at[1]),
    ]
    for c in copies:
        c.start()
    w_local = pltpu.make_async_copy(w_hbm, wbuf.at[x, core, y], lsem.at[2])
    w_stays = (x == p) & (y == x)

    @pl.when(w_stays)
    def _():
        w_local.start()

    barrier = pltpu.get_barrier_semaphore()
    partners = [sib, *y_to, z_up, z_dn, z_far, *x_to, x_two, y_two]
    for d in partners:
        pl.semaphore_signal(barrier, inc=1, device_id=d, device_id_type=MESH)

    @pl.when(jnp.logical_not(w_stays))
    def _():
        pl.semaphore_signal(barrier, inc=1, device_id=dev(p, x, z, core), device_id_type=MESH)

    for yy in range(4):
        @pl.when((x == p) & ((y != x) | (yy != y)))
        def _(yy=yy):
            pl.semaphore_signal(barrier, inc=1, device_id=dev(y, yy, z, core), device_id_type=MESH)

    for c in copies:
        c.wait()
    holds = jnp.where(x == p, 4, 0) + jnp.where(w_stays, -1, 1)
    pl.semaphore_wait(barrier, len(partners) + holds)

    def z_send(t):
        return rc(chunk(p - t, y, core), chunk(p - t, y, core), zs.at[t], zr.at[t + 1], z_up)

    def y_send(t, d):
        return rc(chunk(p - t, y, core), chunk(p - t, y, core), ys.at[d, t], yr.at[d, t], y_to[d])

    def y_got(t, d):
        c = chunk(p - t, (y + 3 - 2 * d) % 4, core)
        return rc(c, c, ys.at[d, t], yr.at[d, t], y_to[d])

    def y_next(t, d):
        c = half(p - t, (y + 3 - 2 * d) % 4, core, d)
        return rc(c, c, ys2.at[d, t], yr2.at[d, t], y_to[d])

    def y_far(t, d):
        c = half(p - t, (y + 2) % 4, core, d)
        return rc(c, c, ys2.at[d, t], yr2.at[d, t], y_to[d])

    def c_send(t, off):
        c = chunk(p - t, (y + off) % 4, core)
        return rc(c, c, cs.at[t, off], cr.at[t, off], sib)

    def c_got(t, off):
        c = chunk(p - t, (y + off) % 4, 1 - core)
        return rc(c, c, cs.at[t, off], cr.at[t, off], sib)

    filled = (p == 3) & (x == 3)

    def z_fill(n):
        c = chunk(2, (y + 2) % 4, core) if n == 2 else half(2, (y + 3 - 2 * n) % 4, core, 1 - n)
        return rc(c, c, zfs.at[n], zfr.at[n], z_up)

    def y_part(yy, d):
        c = half(2, yy, core, d)
        return rc(c, c, ys.at[d, 1], yr.at[d, 1], y_to[d])

    def fill():
        @pl.when((p == 2) & (x == 3))
        def _():
            for n in range(3):
                z_fill(n).start()

    def enter(t):
        @pl.when(p >= t)
        def _():
            if t > 0:
                c = chunk(p - t, y, core)
                rc(c, c, zs.at[t], zr.at[t], z_up).wait_recv()
            if t < 3:
                @pl.when(p < 3)
                def _():
                    z_send(t).start()
            c_send(t, 0).start()
            if t != 1:
                for d in range(2):
                    y_send(t, d).start()

        if t == 1:
            @pl.when((p >= 1) & jnp.logical_not(filled))
            def _():
                for d in range(2):
                    y_send(t, d).start()

            @pl.when(filled)
            def _():
                for d in range(2):
                    y_part(y, d).start()

    def onward(t):
        @pl.when((p >= t) & (jnp.logical_not(filled) | (t != 1)))
        def _():
            for d in range(2):
                y_got(t, d).wait_recv()
                y_next(t, d).start()
                c_send(t, 3 - 2 * d).start()

    def finish(t):
        @pl.when((p >= t) & (jnp.logical_not(filled) | (t != 1)))
        def _():
            for d in range(2):
                y_far(t, d).wait_recv()
            c_send(t, 2).start()

    def fill_take():
        @pl.when(filled)
        def _():
            for d in range(2):
                y_part((y + 3 - 2 * d) % 4, d).wait_recv()
                z_fill(d).wait_recv()
                c_send(1, 3 - 2 * d).start()
            z_fill(2).wait_recv()
            c_send(1, 2).start()

    def w_move():
        return rc(w_hbm, wbuf.at[x, core, y], wxs.at[0], wxr.at[y], dev(p, x, z, core))

    def w_order(i):
        return (i + 2 * (1 - zh)) % 4

    def wz_send(i, d):
        c = wbuf.at[y, core, w_order(i)]
        return rc(c, c, wzs.at[d, i], wzr.at[i], z_up if d == 0 else z_dn)

    def w_pass(i):
        c = wbuf.at[y, core, w_order(i)]

        @pl.when((x == p) & (y == x) & (w_order(i) == y))
        def _():
            w_local.wait()

        @pl.when((x == p) & ((y != x) | (w_order(i) != y)))
        def _():
            rc(c, c, wxs.at[0], wxr.at[w_order(i)], sib).wait_recv()

        @pl.when(x != p)
        def _():
            rc(c, c, wzs.at[0, i], wzr.at[i], sib).wait_recv()

        @pl.when((p >= x) & (p < 3))
        def _():
            wz_send(i, 0).start()

        @pl.when((p <= x) & (p > 0))
        def _():
            wz_send(i, 1).start()

    def w_pass_some(first, last):
        for i in range(first, last):
            w_pass(i)

    def w_take(i):
        c = wbuf.at[y, core, w_order(i)]
        rc(c, c, wzs.at[0, i], wzr.at[i], sib).wait_recv()

    def w_half(yy, c_, k):
        return wbuf.at[yy, c_, pl.ds(2 * ((1 - zh + k) % 2), 2)]

    def wy_send(k, d):
        c = w_half(y, core, k)
        return rc(c, c, wys.at[d, k], wyr.at[d, k], y_to[d])

    def wy_got(k, d):
        c = w_half((y + 3 - 2 * d) % 4, core, k)
        return rc(c, c, wys.at[d, k], wyr.at[d, k], y_to[d])

    def wy_next(k, d):
        c = wbuf.at[(y + 3 - 2 * d) % 4, core, 2 * ((1 - zh + k) % 2) + d]
        return rc(c, c, wys2.at[d, k], wyr2.at[d, k], y_to[d])

    def wy_far(k, d):
        c = wbuf.at[(y + 2) % 4, core, 2 * ((1 - zh + k) % 2) + d]
        return rc(c, c, wys2.at[d, k], wyr2.at[d, k], y_to[d])

    def wc(k, off, c_):
        c = w_half((y + off) % 4, c_, k)
        return rc(c, c, wcs.at[k, off], wcr.at[k, off], sib)

    def w_enter(k):
        for d in range(2):
            wy_send(k, d).start()
        wc(k, 0, core).start()

    def w_onward(k):
        for d in range(2):
            wy_got(k, d).wait_recv()
            wy_next(k, d).start()
            wc(k, 3 - 2 * d, core).start()

    def w_finish(k):
        for d in range(2):
            wy_far(k, d).wait_recv()
        wc(k, 2, core).start()

    def w_done(k):
        for off in range(4):
            wc(k, off, 1 - core).wait_recv()

    @pl.when(jnp.logical_not(w_stays))
    def _():
        w_move().start()

    enter(0)

    kvbuf[0:4] = jnp.zeros((4, 2, BLOCK, HEAD_DIM), jnp.bfloat16)

    def mask_step(n, carry):
        m, strip = n // 4, n % 4
        i = lax.broadcasted_iota(jnp.int32, (32, WIN), 0) + strip * 32
        j = lax.broadcasted_iota(jnp.int32, (32, WIN), 1)
        d = 4 * BLOCK + i - j
        b = jnp.where(d == 0, 0.0, NEG)
        for e in range(NS):
            b = jnp.where(d == slash[e, kv * GROUP + m] + 1, 0.0, b)
        sbias[m, pl.ds(pl.multiple_of(strip * 32, 32), 32), :] = b
        return carry

    lax.fori_loop(0, 16, mask_step, 0)

    @pl.when(((p == 0) & (x == 0)) | ((p == 3) & (x == 3)))
    def _():
        w_pass_some(0, 4)

    enter(1)

    @pl.when(p == 1)
    def _():
        w_pass_some(0, 4)

    @pl.when((p == 2) & (x >= 2))
    def _():
        w_pass_some(0, 2)

    onward(0)
    enter(2)

    @pl.when((p == 2) & (x >= 2))
    def _():
        w_pass_some(2, 4)

    @pl.when((p == 2) & (x < 2))
    def _():
        w_pass_some(0, 4)

    onward(1)
    finish(0)
    fill()
    enter(3)
    onward(2)
    finish(1)
    onward(3)

    @pl.when((p == 3) & (x < 3))
    def _():
        w_take(0)
        w_take(1)

    fill_take()
    w_late = (p == 0) & (x > 0)

    @pl.when(jnp.logical_not(w_late))
    def _():
        w_enter(0)

    finish(2)
    finish(3)

    @pl.when((p == 3) & (x < 3))
    def _():
        w_take(2)
        w_take(3)

    @pl.when(jnp.logical_not(w_late))
    def _():
        w_enter(1)

    for t in range(4):
        @pl.when(p >= t)
        def _(t=t):
            for off in range(4):
                c_got(t, off).wait_recv()

    wi = lax.broadcasted_iota(jnp.int32, (BLOCK, WIN), 0)
    wj = lax.broadcasted_iota(jnp.int32, (BLOCK, WIN), 1)
    lane = lax.broadcasted_iota(jnp.int32, (1, WIN), 1)

    def attend(r):
        rows = pl.ds(pl.multiple_of(r * BLOCK, BLOCK), BLOCK)
        here = 4 * seq + r
        kw = kvbuf[pl.ds(here, 5), 0].reshape(WIN, HEAD_DIM)
        vw = kvbuf[pl.ds(here, 5), 1].reshape(WIN, HEAD_DIM)
        vw = jnp.concatenate([vw, jnp.ones((WIN, HEAD_DIM), jnp.bfloat16)], axis=1)
        ones = jnp.ones((PICK, HEAD_DIM), jnp.bfloat16)
        bcol = here - 4 + lane // BLOCK
        alt = jnp.where((wj >= 4 * BLOCK) & (wi >= wj - 4 * BLOCK), 0.0, NEG)
        for m in range(GROUP):
            q = q_ref[rows, m * HEAD_DIM : (m + 1) * HEAD_DIM]
            oncol = bcol <= 0
            pb = [jnp.full((1, BLOCK), jnp.where(here > 0, 0.0, NEG), jnp.float32)]
            at = [4]
            for e in range(NV):
                b = vert[e, kv * GROUP + m] + 1
                oncol = oncol | (bcol == b)
                pb.append(jnp.full((1, BLOCK), jnp.where(b < here, 0.0, NEG), jnp.float32))
                at.append(4 + jnp.where(b < here, b, 0))
            kp = jnp.concatenate([kvbuf[a, 0] for a in at], axis=0)
            vp = jnp.concatenate([kvbuf[a, 1] for a in at], axis=0)
            sw = dot_t(q, kw) + jnp.where(oncol, alt, sbias[m])
            sp = dot_t(q, kp) + jnp.concatenate(pb, axis=1)
            peak = jnp.maximum(
                jnp.max(sw, axis=1, keepdims=True), jnp.max(sp, axis=1, keepdims=True)
            )
            pw = jnp.exp2((sw - peak) * SCALE).astype(jnp.bfloat16)
            pp = jnp.exp2((sp - peak) * SCALE).astype(jnp.bfloat16)
            o = dot(pw, vw) + dot(pp, jnp.concatenate([vp, ones], axis=1))
            abuf[x, r, m] = (o[:, :HEAD_DIM] / o[:, HEAD_DIM:]).astype(jnp.bfloat16)

    def a_part(xx, r, m):
        return abuf.at[xx, r, pl.ds(m - UNIT + 1, UNIT)]

    def x_copy(c, ss, rs, r, m, d):
        n = r * GROUP + m
        return rc(c, c, ss.at[d, n], rs.at[d, n], x_to[d])

    def x_send(r, m, d):
        return x_copy(a_part(x, r, m), xs, xr, r, m, d)

    def x_got(r, m, d):
        return x_copy(a_part((x + 3 - 2 * d) % 4, r, m), xs, xr, r, m, d)

    def x_far(xx, r, m):
        c = a_part(xx, r, m)
        n = r * GROUP + m
        return rc(c, c, xs2.at[n], xr2.at[n], x_two)

    def e_send(r, d):
        c = pl.ds(d * 64, 64)
        return rc(zsrc.at[r, c], zdst.at[r, c], es.at[d, r], er.at[d, r], z_far)

    def product(r, h):
        acc = None
        for i in range(4):
            w = jnp.concatenate(
                [wbuf[i, n % 2, 2 * h + n // 2] for n in range(4)], axis=1
            )
            a = jnp.concatenate([abuf[i, r, m] for m in range(GROUP)], axis=1)
            part = dot(a, w)
            acc = part if acc is None else acc + part
        return acc

    ends = range(UNIT - 1, GROUP, UNIT)

    def step(it, carry):
        @pl.when(it < RBLK)
        def _():
            attend(it)
            for m in ends:
                for d in range(2):
                    x_send(it, m, d).start()
                x_far(x, it, m).start()

        @pl.when((it == LATE) & w_late)
        def _():
            w_take(0)
            w_take(1)
            w_enter(0)
            w_take(2)
            w_take(3)
            w_enter(1)

        for at, act, k in W_STEPS:
            @pl.when(it == at)
            def _(act=act, k=k):
                (w_onward, w_finish, w_done)[act](k)

        @pl.when((it >= LAG2) & (it < RBLK + LAG2))
        def _():
            r = it - LAG2
            for m in ends:
                for d in range(2):
                    x_got(r, m, d).wait_recv()
                x_far((x + 2) % 4, r, m).wait_recv()
            zsrc[r] = product(r, 1 - zh).astype(jnp.bfloat16)
            for d in range(2):
                e_send(r, d).start()

        for at, act, k in W_LATER:
            @pl.when(it == at)
            def _(act=act, k=k):
                (w_onward, w_finish, w_done)[act](k)

        @pl.when(it >= LAG3)
        def _():
            r = it - LAG3
            mine = product(r, zh)
            for d in range(2):
                e_send(r, d).wait_recv()
            rows = pl.ds(pl.multiple_of(r * BLOCK, BLOCK), BLOCK)
            out_ref[rows, :] = (mine + zdst[r].astype(jnp.float32)).astype(jnp.bfloat16)

        return carry

    lax.fori_loop(0, RBLK + LAG3, step, 0)

    for t in range(4):
        @pl.when(p >= t)
        def _(t=t):
            if t < 3:
                @pl.when(p < 3)
                def _():
                    z_send(t).wait_send()
            for off in range(4):
                c_send(t, off).wait_send()

        @pl.when((p >= t) & (jnp.logical_not(filled) | (t != 1)))
        def _(t=t):
            for d in range(2):
                y_send(t, d).wait_send()
                y_next(t, d).wait_send()

    @pl.when(filled)
    def _():
        for d in range(2):
            y_part(y, d).wait_send()

    @pl.when((p == 2) & (x == 3))
    def _():
        for n in range(3):
            z_fill(n).wait_send()

    @pl.when(jnp.logical_not(w_stays))
    def _():
        w_move().wait_send()

    for i in range(4):
        @pl.when((p >= x) & (p < 3))
        def _(i=i):
            wz_send(i, 0).wait_send()

        @pl.when((p <= x) & (p > 0))
        def _(i=i):
            wz_send(i, 1).wait_send()

    for k in range(2):
        for d in range(2):
            wy_send(k, d).wait_send()
            wy_next(k, d).wait_send()
        for off in range(4):
            wc(k, off, core).wait_send()

    def drain(r, carry):
        for d in range(2):
            for m in range(UNIT - 1, GROUP, UNIT):
                x_send(r, m, d).wait_send()
            e_send(r, d).wait_send()
        for m in ends:
            x_far(x, r, m).wait_send()
        return carry

    lax.fori_loop(0, 4, drain, 0)


def shards(queries, key_rows, value_rows, out_weight, vertical, slash_offsets):
    bf16 = jnp.bfloat16
    dma = pltpu.SemaphoreType.DMA
    smem = pl.BlockSpec(memory_space=pltpu.SMEM)
    vmem = pl.BlockSpec(memory_space=pltpu.VMEM)
    anyspace = pl.BlockSpec(memory_space=pl.ANY)
    return pl.pallas_call(
        kernel,
        out_shape=jax.ShapeDtypeStruct((ROWS, ROWS), bf16),
        in_specs=[smem, smem, vmem, anyspace, anyspace, anyspace],
        out_specs=vmem,
        scratch_shapes=[
            pltpu.VMEM((132, 2, BLOCK, HEAD_DIM), bf16),
            pltpu.VMEM((4, 2, 4, ROWS, 128), bf16),
            pltpu.VMEM((4, RBLK, GROUP, BLOCK, HEAD_DIM), bf16),
            pltpu.VMEM((GROUP, BLOCK, WIN), jnp.float32),
            pltpu.VMEM((RBLK, BLOCK, ROWS), bf16),
            pltpu.VMEM((RBLK, BLOCK, ROWS), bf16),
            dma((3,)),
            dma((4,)), dma((4,)), dma((3,)), dma((3,)),
            dma((2, 4)), dma((2, 4)), dma((2, 4)), dma((2, 4)),
            dma((4, 4)), dma((4, 4)),
            dma((1,)), dma((4,)),
            dma((2, 4)), dma((4,)),
            dma((2, 2)), dma((2, 2)), dma((2, 2)), dma((2, 2)),
            dma((2, 4)), dma((2, 4)),
            dma((2, 16)), dma((2, 16)), dma((16,)), dma((16,)),
            dma((2, 4)), dma((2, 4)),
        ],
        compiler_params=pltpu.CompilerParams(
            collective_id=0, has_side_effects=True, vmem_limit_bytes=56 * 1024 * 1024
        ),
    )(
        vertical.T,
        slash_offsets.T,
        queries,
        key_rows.reshape(4, BLOCK, HEAD_DIM),
        value_rows.reshape(4, BLOCK, HEAD_DIM),
        out_weight,
    )


def solution(mesh):
    in_specs = (P("seq", "kv"), P("seq", "kv"), P("seq", "kv"), P("kv", "seq"), P(), P())
    out_specs = P("seq", "kv")
    return jax.shard_map(shards, mesh=mesh, in_specs=in_specs, out_specs=out_specs, check_vma=False)
```

```python
import functools
import math

import jax
import jax.numpy as jnp
from jax import lax
from jax.experimental import pallas as pl
from jax.experimental.pallas import tpu as pltpu
from jax.sharding import PartitionSpec as P

MESH = pl.DeviceIdType.MESH
HEAD_DIM = 128
BLOCK = 128
GROUP = 4
ROWS = 512
NV = 16
NS = 16
NPICK = NV + 1
RBLK = ROWS // BLOCK
WIN = 5 * BLOCK
PICK = NPICK * BLOCK
NEG = -1e30
UNIT = 2
LAG2 = 2
LAG3 = 6
LATE = 0
W_STEPS = [(1, 0, 0), (2, 1, 0), (2, 2, 0)]
W_LATER = [(3, 0, 1), (4, 1, 1), (5, 2, 1)]
SCALE = math.log2(math.e) / math.sqrt(HEAD_DIM)


def dot(a, b):
    return jnp.dot(a, b, preferred_element_type=jnp.float32)


def dot_t(a, b):
    return lax.dot_general(a, b, (((1,), (1,)), ((), ())), preferred_element_type=jnp.float32)


def kernel(
    vert, slash, q_hbm, k_hbm, v_hbm, w_hbm, out_ref,
    q_ref, kvbuf, wbuf, abuf, sbias, zsrc, zdst,
    lsem, zs, zr, zfs, zfr, ys, yr, ys2, yr2, cs, cr,
    wxs, wxr, wzs, wzr, wys, wyr, wys2, wyr2, wcs, wcr,
    xs, xr, xs2, xr2, es, er,
):
    seq = lax.axis_index("seq")
    kv = lax.axis_index("kv")
    core = seq % 2
    y = (seq // 2) % 4
    p = seq // 8
    x = kv // 2
    zh = kv % 2
    z = zh * 4 + p

    def dev(x_, y_, z_, c_):
        return (((z_ % 4) * 4 + y_) * 2 + c_, x_ * 2 + z_ // 4)

    sib = dev(x, y, z, 1 - core)
    y_to = [dev(x, (y + 1) % 4, z, core), dev(x, (y + 3) % 4, z, core)]
    x_two = dev((x + 2) % 4, y, z, core)
    z_up = dev(x, y, (z + 1) % 8, core)
    z_dn = dev(x, y, (z + 7) % 8, core)
    z_far = dev(x, y, (z + 4) % 8, core)
    x_to = [dev((x + 1) % 4, y, z, core), dev((x + 3) % 4, y, z, core)]

    def rc(src, dst, ss, rs, d):
        return pltpu.make_async_remote_copy(
            src_ref=src, dst_ref=dst, send_sem=ss, recv_sem=rs, device_id=d, device_id_type=MESH
        )

    def chunk(q, yy, c):
        return kvbuf.at[pl.ds(4 + 4 * ((q * 4 + yy) * 2 + c), 4)]

    def half(q, yy, c, h):
        return kvbuf.at[pl.ds(4 + 4 * ((q * 4 + yy) * 2 + c) + 2 * h, 2)]

    base = 4 + 4 * seq
    copies = [
        pltpu.make_async_copy(k_hbm, kvbuf.at[pl.ds(base, 4), 0], lsem.at[0]),
        pltpu.make_async_copy(v_hbm, kvbuf.at[pl.ds(base, 4), 1], lsem.at[1]),
    ]
    for c in copies:
        c.start()
    q_copy = pltpu.make_async_copy(q_hbm, q_ref, lsem.at[3])
    q_copy.start()
    w_local = pltpu.make_async_copy(w_hbm, wbuf.at[x, core, y], lsem.at[2])
    w_stays = (x == p) & (y == x)

    @pl.when(w_stays)
    def _():
        w_local.start()

    barrier = pltpu.get_barrier_semaphore()
    partners = [sib, *y_to, z_up, z_dn, z_far, *x_to, x_two]
    for d in partners:
        pl.semaphore_signal(barrier, inc=1, device_id=d, device_id_type=MESH)

    @pl.when(jnp.logical_not(w_stays))
    def _():
        pl.semaphore_signal(barrier, inc=1, device_id=dev(p, x, z, core), device_id_type=MESH)

    for yy in range(4):
        @pl.when((x == p) & ((y != x) | (yy != y)))
        def _(yy=yy):
            pl.semaphore_signal(barrier, inc=1, device_id=dev(y, yy, z, core), device_id_type=MESH)

    for c in copies:
        c.wait()
    holds = jnp.where(x == p, 4, 0) + jnp.where(w_stays, -1, 1)
    pl.semaphore_wait(barrier, len(partners) + holds)

    def z_send(t):
        return rc(chunk(p - t, y, core), chunk(p - t, y, core), zs.at[t], zr.at[t + 1], z_up)

    def y_send(t, d):
        return rc(chunk(p - t, y, core), chunk(p - t, y, core), ys.at[d, t], yr.at[d, t], y_to[d])

    def y_got(t, d):
        c = chunk(p - t, (y + 3 - 2 * d) % 4, core)
        return rc(c, c, ys.at[d, t], yr.at[d, t], y_to[d])

    def y_next(t, d):
        c = half(p - t, (y + 3 - 2 * d) % 4, core, d)
        return rc(c, c, ys2.at[d, t], yr2.at[d, t], y_to[d])

    def y_far(t, d):
        c = half(p - t, (y + 2) % 4, core, d)
        return rc(c, c, ys2.at[d, t], yr2.at[d, t], y_to[d])

    def c_send(t, off):
        c = chunk(p - t, (y + off) % 4, core)
        return rc(c, c, cs.at[t, off], cr.at[t, off], sib)

    def c_got(t, off):
        c = chunk(p - t, (y + off) % 4, 1 - core)
        return rc(c, c, cs.at[t, off], cr.at[t, off], sib)

    filled = (p == 3) & (x == 3)

    def z_fill(n):
        c = chunk(2, (y + (3, 1, 2)[n]) % 4, core)
        return rc(c, c, zfs.at[n], zfr.at[n], z_up)

    def fill():
        @pl.when(p == 2)
        def _():
            z_fill(2).start()

        @pl.when((p == 2) & (x == 3))
        def _():
            for n in range(2):
                z_fill(n).start()

    def enter(t):
        @pl.when(p >= t)
        def _():
            if t > 0:
                c = chunk(p - t, y, core)
                rc(c, c, zs.at[t], zr.at[t], z_up).wait_recv()
            if t < 3:
                @pl.when(p < 3)
                def _():
                    z_send(t).start()
            c_send(t, 0).start()
            if t != 1:
                for d in range(2):
                    y_send(t, d).start()

        if t == 1:
            @pl.when((p >= 1) & jnp.logical_not(filled))
            def _():
                for d in range(2):
                    y_send(t, d).start()

    def onward(t):
        @pl.when((p >= t) & (jnp.logical_not(filled) | (t != 1)))
        def _():
            for d in range(2):
                y_got(t, d).wait_recv()

                @pl.when((p < 3) | (t != 1))
                def _(d=d):
                    y_next(t, d).start()

                c_send(t, 3 - 2 * d).start()

    def finish(t):
        @pl.when((p >= t) & ((p < 3) | (t != 1)))
        def _():
            for d in range(2):
                y_far(t, d).wait_recv()
            c_send(t, 2).start()

    def fill_take():
        @pl.when(filled)
        def _():
            for d in range(2):
                z_fill(d).wait_recv()
                c_send(1, 3 - 2 * d).start()

        @pl.when(p == 3)
        def _():
            z_fill(2).wait_recv()
            c_send(1, 2).start()

    def w_move():
        return rc(w_hbm, wbuf.at[x, core, y], wxs.at[0], wxr.at[y], dev(p, x, z, core))

    def w_order(i):
        return (i + 2 * (1 - zh)) % 4

    def wz_send(i, d):
        c = wbuf.at[y, core, w_order(i)]
        return rc(c, c, wzs.at[d, i], wzr.at[i], z_up if d == 0 else z_dn)

    def w_pass(i):
        c = wbuf.at[y, core, w_order(i)]

        @pl.when((x == p) & (y == x) & (w_order(i) == y))
        def _():
            w_local.wait()

        @pl.when((x == p) & ((y != x) | (w_order(i) != y)))
        def _():
            rc(c, c, wxs.at[0], wxr.at[w_order(i)], sib).wait_recv()

        @pl.when(x != p)
        def _():
            rc(c, c, wzs.at[0, i], wzr.at[i], sib).wait_recv()

        @pl.when((p >= x) & (p < 3))
        def _():
            wz_send(i, 0).start()

        @pl.when((p <= x) & (p > 0))
        def _():
            wz_send(i, 1).start()

    def w_pass_some(first, last):
        for i in range(first, last):
            w_pass(i)

    def w_take(i):
        c = wbuf.at[y, core, w_order(i)]
        rc(c, c, wzs.at[0, i], wzr.at[i], sib).wait_recv()

    def w_half(yy, c_, k):
        return wbuf.at[yy, c_, pl.ds(2 * ((1 - zh + k) % 2), 2)]

    def wy_send(k, d):
        c = w_half(y, core, k)
        return rc(c, c, wys.at[d, k], wyr.at[d, k], y_to[d])

    def wy_got(k, d):
        c = w_half((y + 3 - 2 * d) % 4, core, k)
        return rc(c, c, wys.at[d, k], wyr.at[d, k], y_to[d])

    def wy_next(k, d):
        c = wbuf.at[(y + 3 - 2 * d) % 4, core, 2 * ((1 - zh + k) % 2) + d]
        return rc(c, c, wys2.at[d, k], wyr2.at[d, k], y_to[d])

    def wy_far(k, d):
        c = wbuf.at[(y + 2) % 4, core, 2 * ((1 - zh + k) % 2) + d]
        return rc(c, c, wys2.at[d, k], wyr2.at[d, k], y_to[d])

    def wc(k, off, c_):
        c = w_half((y + off) % 4, c_, k)
        return rc(c, c, wcs.at[k, off], wcr.at[k, off], sib)

    def w_enter(k):
        for d in range(2):
            wy_send(k, d).start()
        wc(k, 0, core).start()

    def w_onward(k):
        for d in range(2):
            wy_got(k, d).wait_recv()
            wy_next(k, d).start()
            wc(k, 3 - 2 * d, core).start()

    def w_finish(k):
        for d in range(2):
            wy_far(k, d).wait_recv()
        wc(k, 2, core).start()

    def w_done(k):
        for off in range(4):
            wc(k, off, 1 - core).wait_recv()

    @pl.when(jnp.logical_not(w_stays))
    def _():
        w_move().start()

    enter(0)

    kvbuf[0:4] = jnp.zeros((4, 2, BLOCK, HEAD_DIM), jnp.bfloat16)

    def mask_step(n, carry):
        m, strip = n // 4, n % 4
        i = lax.broadcasted_iota(jnp.int32, (32, WIN), 0) + strip * 32
        j = lax.broadcasted_iota(jnp.int32, (32, WIN), 1)
        d = 4 * BLOCK + i - j
        b = jnp.where(d == 0, 0.0, NEG)
        for e in range(NS):
            b = jnp.where(d == slash[e, kv * GROUP + m] + 1, 0.0, b)
        sbias[m, pl.ds(pl.multiple_of(strip * 32, 32), 32), :] = b
        return carry

    lax.fori_loop(0, 16, mask_step, 0)

    @pl.when(((p == 0) & (x == 0)) | ((p == 3) & (x == 3)))
    def _():
        w_pass_some(0, 4)

    enter(1)

    @pl.when((p == 1) & (x < 2))
    def _():
        w_pass_some(0, 4)

    @pl.when((p == 2) & (x >= 2))
    def _():
        w_pass_some(0, 2)

    onward(0)
    enter(2)

    @pl.when((p == 2) & (x >= 2))
    def _():
        w_pass_some(2, 4)

    @pl.when((p == 2) & (x < 2))
    def _():
        w_pass_some(0, 4)

    onward(1)
    finish(0)

    @pl.when((p == 1) & (x >= 2))
    def _():
        w_pass_some(0, 4)

    fill()
    enter(3)
    onward(2)
    finish(1)
    onward(3)

    @pl.when((p == 3) & (x < 3))
    def _():
        w_take(0)
        w_take(1)

    fill_take()
    w_late = (p == 0) & (x > 0)

    @pl.when(jnp.logical_not(w_late))
    def _():
        w_enter(0)

    finish(2)
    finish(3)

    @pl.when((p == 3) & (x < 3))
    def _():
        w_take(2)
        w_take(3)

    @pl.when(jnp.logical_not(w_late))
    def _():
        w_enter(1)

    for t in range(4):
        @pl.when(p >= t)
        def _(t=t):
            for off in range(4):
                c_got(t, off).wait_recv()

    q_copy.wait()
    wi = lax.broadcasted_iota(jnp.int32, (BLOCK, WIN), 0)
    wj = lax.broadcasted_iota(jnp.int32, (BLOCK, WIN), 1)
    lane = lax.broadcasted_iota(jnp.int32, (1, WIN), 1)

    def attend(r):
        rows = pl.ds(pl.multiple_of(r * BLOCK, BLOCK), BLOCK)
        here = 4 * seq + r
        kw = kvbuf[pl.ds(here, 5), 0].reshape(WIN, HEAD_DIM)
        vw = kvbuf[pl.ds(here, 5), 1].reshape(WIN, HEAD_DIM)
        vw = jnp.concatenate([vw, jnp.ones((WIN, HEAD_DIM), jnp.bfloat16)], axis=1)
        ones = jnp.ones((PICK, HEAD_DIM), jnp.bfloat16)
        bcol = here - 4 + lane // BLOCK
        alt = jnp.where((wj >= 4 * BLOCK) & (wi >= wj - 4 * BLOCK), 0.0, NEG)
        for m in range(GROUP):
            q = q_ref[rows, m * HEAD_DIM : (m + 1) * HEAD_DIM]
            oncol = bcol <= 0
            pb = [jnp.full((1, BLOCK), jnp.where(here > 0, 0.0, NEG), jnp.float32)]
            at = [4]
            for e in range(NV):
                b = vert[e, kv * GROUP + m] + 1
                oncol = oncol | (bcol == b)
                pb.append(jnp.full((1, BLOCK), jnp.where(b < here, 0.0, NEG), jnp.float32))
                at.append(4 + jnp.where(b < here, b, 0))
            kp = jnp.concatenate([kvbuf[a, 0] for a in at], axis=0)
            vp = jnp.concatenate([kvbuf[a, 1] for a in at], axis=0)
            sw = dot_t(q, kw) + jnp.where(oncol, alt, sbias[m])
            sp = dot_t(q, kp) + jnp.concatenate(pb, axis=1)
            peak = jnp.maximum(
                jnp.max(sw, axis=1, keepdims=True), jnp.max(sp, axis=1, keepdims=True)
            )
            pw = jnp.exp2((sw - peak) * SCALE).astype(jnp.bfloat16)
            pp = jnp.exp2((sp - peak) * SCALE).astype(jnp.bfloat16)
            o = dot(pw, vw) + dot(pp, jnp.concatenate([vp, ones], axis=1))
            abuf[x, r, m] = (o[:, :HEAD_DIM] / o[:, HEAD_DIM:]).astype(jnp.bfloat16)

    def a_part(xx, r, m):
        return abuf.at[xx, r, pl.ds(m - UNIT + 1, UNIT)]

    def x_copy(c, ss, rs, r, m, d):
        n = r * GROUP + m
        return rc(c, c, ss.at[d, n], rs.at[d, n], x_to[d])

    def x_send(r, m, d):
        return x_copy(a_part(x, r, m), xs, xr, r, m, d)

    def x_got(r, m, d):
        return x_copy(a_part((x + 3 - 2 * d) % 4, r, m), xs, xr, r, m, d)

    def x_far(xx, r, m):
        c = a_part(xx, r, m)
        n = r * GROUP + m
        return rc(c, c, xs2.at[n], xr2.at[n], x_two)

    def e_send(r, d):
        c = pl.ds(d * 64, 64)
        return rc(zsrc.at[r, c], zdst.at[r, c], es.at[d, r], er.at[d, r], z_far)

    def product(r, h):
        acc = None
        for i in range(4):
            w = jnp.concatenate(
                [wbuf[i, n % 2, 2 * h + n // 2] for n in range(4)], axis=1
            )
            a = jnp.concatenate([abuf[i, r, m] for m in range(GROUP)], axis=1)
            part = dot(a, w)
            acc = part if acc is None else acc + part
        return acc

    ends = range(UNIT - 1, GROUP, UNIT)

    def step(it, carry):
        @pl.when(it < RBLK)
        def _():
            attend(it)
            for m in ends:
                for d in range(2):
                    x_send(it, m, d).start()
                x_far(x, it, m).start()

        @pl.when((it == LATE) & w_late)
        def _():
            w_take(0)
            w_take(1)
            w_enter(0)
            w_take(2)
            w_take(3)
            w_enter(1)

        for at, act, k in W_STEPS:
            @pl.when(it == at)
            def _(act=act, k=k):
                (w_onward, w_finish, w_done)[act](k)

        @pl.when((it >= LAG2) & (it < RBLK + LAG2))
        def _():
            r = it - LAG2
            for m in ends:
                for d in range(2):
                    x_got(r, m, d).wait_recv()
                x_far((x + 2) % 4, r, m).wait_recv()
            zsrc[r] = product(r, 1 - zh).astype(jnp.bfloat16)
            for d in range(2):
                e_send(r, d).start()

        for at, act, k in W_LATER:
            @pl.when(it == at)
            def _(act=act, k=k):
                (w_onward, w_finish, w_done)[act](k)

        @pl.when(it >= LAG3)
        def _():
            r = it - LAG3
            mine = product(r, zh)
            for d in range(2):
                e_send(r, d).wait_recv()
            rows = pl.ds(pl.multiple_of(r * BLOCK, BLOCK), BLOCK)
            out_ref[rows, :] = (mine + zdst[r].astype(jnp.float32)).astype(jnp.bfloat16)

        return carry

    lax.fori_loop(0, RBLK + LAG3, step, 0)

    for t in range(4):
        @pl.when(p >= t)
        def _(t=t):
            if t < 3:
                @pl.when(p < 3)
                def _():
                    z_send(t).wait_send()
            for off in range(4):
                c_send(t, off).wait_send()

        @pl.when((p >= t) & (jnp.logical_not(filled) | (t != 1)))
        def _(t=t):
            for d in range(2):
                y_send(t, d).wait_send()

        @pl.when((p >= t) & ((p < 3) | (t != 1)))
        def _(t=t):
            for d in range(2):
                y_next(t, d).wait_send()

    @pl.when(p == 2)
    def _():
        z_fill(2).wait_send()

    @pl.when((p == 2) & (x == 3))
    def _():
        for n in range(2):
            z_fill(n).wait_send()

    @pl.when(jnp.logical_not(w_stays))
    def _():
        w_move().wait_send()

    for i in range(4):
        @pl.when((p >= x) & (p < 3))
        def _(i=i):
            wz_send(i, 0).wait_send()

        @pl.when((p <= x) & (p > 0))
        def _(i=i):
            wz_send(i, 1).wait_send()

    for k in range(2):
        for d in range(2):
            wy_send(k, d).wait_send()
            wy_next(k, d).wait_send()
        for off in range(4):
            wc(k, off, core).wait_send()

    def drain(r, carry):
        for d in range(2):
            for m in range(UNIT - 1, GROUP, UNIT):
                x_send(r, m, d).wait_send()
            e_send(r, d).wait_send()
        for m in ends:
            x_far(x, r, m).wait_send()
        return carry

    lax.fori_loop(0, 4, drain, 0)


def shards(queries, key_rows, value_rows, out_weight, vertical, slash_offsets):
    bf16 = jnp.bfloat16
    dma = pltpu.SemaphoreType.DMA
    smem = pl.BlockSpec(memory_space=pltpu.SMEM)
    vmem = pl.BlockSpec(memory_space=pltpu.VMEM)
    anyspace = pl.BlockSpec(memory_space=pl.ANY)
    return pl.pallas_call(
        kernel,
        out_shape=jax.ShapeDtypeStruct((ROWS, ROWS), bf16),
        in_specs=[smem, smem, anyspace, anyspace, anyspace, anyspace],
        out_specs=vmem,
        scratch_shapes=[
            pltpu.VMEM((ROWS, GROUP * HEAD_DIM), bf16),
            pltpu.VMEM((132, 2, BLOCK, HEAD_DIM), bf16),
            pltpu.VMEM((4, 2, 4, ROWS, 128), bf16),
            pltpu.VMEM((4, RBLK, GROUP, BLOCK, HEAD_DIM), bf16),
            pltpu.VMEM((GROUP, BLOCK, WIN), jnp.float32),
            pltpu.VMEM((RBLK, BLOCK, ROWS), bf16),
            pltpu.VMEM((RBLK, BLOCK, ROWS), bf16),
            dma((4,)),
            dma((4,)), dma((4,)), dma((3,)), dma((3,)),
            dma((2, 4)), dma((2, 4)), dma((2, 4)), dma((2, 4)),
            dma((4, 4)), dma((4, 4)),
            dma((1,)), dma((4,)),
            dma((2, 4)), dma((4,)),
            dma((2, 2)), dma((2, 2)), dma((2, 2)), dma((2, 2)),
            dma((2, 4)), dma((2, 4)),
            dma((2, 16)), dma((2, 16)), dma((16,)), dma((16,)),
            dma((2, 4)), dma((2, 4)),
        ],
        compiler_params=pltpu.CompilerParams(
            collective_id=0, has_side_effects=True, vmem_limit_bytes=56 * 1024 * 1024
        ),
    )(
        vertical.T,
        slash_offsets.T,
        queries,
        key_rows.reshape(4, BLOCK, HEAD_DIM),
        value_rows.reshape(4, BLOCK, HEAD_DIM),
        out_weight,
    )


def solution(mesh):
    in_specs = (P("seq", "kv"), P("seq", "kv"), P("seq", "kv"), P("kv", "seq"), P(), P())
    out_specs = P("seq", "kv")
    return jax.shard_map(shards, mesh=mesh, in_specs=in_specs, out_specs=out_specs, check_vma=False)
```

```python
import functools
import math

import jax
import jax.numpy as jnp
from jax import lax
from jax.experimental import pallas as pl
from jax.experimental.pallas import tpu as pltpu
from jax.sharding import PartitionSpec as P

MESH = pl.DeviceIdType.MESH
HEAD_DIM = 128
BLOCK = 128
GROUP = 4
ROWS = 512
NV = 16
NS = 16
NPICK = NV + 1
RBLK = ROWS // BLOCK
WIN = 5 * BLOCK
PICK = NPICK * BLOCK
NEG = -1e30
UNIT = 4
LAG2 = 2
LAG3 = 6
LATE = 0
W_STEPS = [(1, 0, 0), (2, 1, 0), (2, 2, 0)]
W_LATER = [(3, 0, 1), (4, 1, 1), (5, 2, 1)]
SCALE = math.log2(math.e) / math.sqrt(HEAD_DIM)


def dot(a, b):
    return jnp.dot(a, b, preferred_element_type=jnp.float32)


def dot_t(a, b):
    return lax.dot_general(a, b, (((1,), (1,)), ((), ())), preferred_element_type=jnp.float32)


def kernel(
    vert, slash, q_hbm, k_hbm, v_hbm, w_hbm, out_ref,
    q_ref, kvbuf, wbuf, abuf, sbias, zsrc, zdst,
    lsem, zs, zr, zfs, zfr, ys, yr, ys2, yr2, cs, cr,
    wxs, wxr, wzs, wzr, wys, wyr, wys2, wyr2, wcs, wcr,
    xs, xr, xs2, xr2, es, er,
):
    seq = lax.axis_index("seq")
    kv = lax.axis_index("kv")
    core = seq % 2
    y = (seq // 2) % 4
    p = seq // 8
    x = kv // 2
    zh = kv % 2
    z = zh * 4 + p

    def dev(x_, y_, z_, c_):
        return (((z_ % 4) * 4 + y_) * 2 + c_, x_ * 2 + z_ // 4)

    sib = dev(x, y, z, 1 - core)
    y_to = [dev(x, (y + 1) % 4, z, core), dev(x, (y + 3) % 4, z, core)]
    x_two = dev((x + 2) % 4, y, z, core)
    z_up = dev(x, y, (z + 1) % 8, core)
    z_dn = dev(x, y, (z + 7) % 8, core)
    z_far = dev(x, y, (z + 4) % 8, core)
    x_to = [dev((x + 1) % 4, y, z, core), dev((x + 3) % 4, y, z, core)]

    def rc(src, dst, ss, rs, d):
        return pltpu.make_async_remote_copy(
            src_ref=src, dst_ref=dst, send_sem=ss, recv_sem=rs, device_id=d, device_id_type=MESH
        )

    def chunk(q, yy, c):
        return kvbuf.at[pl.ds(4 + 4 * ((q * 4 + yy) * 2 + c), 4)]

    def half(q, yy, c, h):
        return kvbuf.at[pl.ds(4 + 4 * ((q * 4 + yy) * 2 + c) + 2 * h, 2)]

    base = 4 + 4 * seq
    copies = [
        pltpu.make_async_copy(k_hbm, kvbuf.at[pl.ds(base, 4), 0], lsem.at[0]),
        pltpu.make_async_copy(v_hbm, kvbuf.at[pl.ds(base, 4), 1], lsem.at[1]),
    ]
    for c in copies:
        c.start()
    q_copy = pltpu.make_async_copy(q_hbm, q_ref, lsem.at[3])
    q_copy.start()
    w_local = pltpu.make_async_copy(w_hbm, wbuf.at[x, core, y], lsem.at[2])
    w_stays = (x == p) & (y == x)

    @pl.when(w_stays)
    def _():
        w_local.start()

    barrier = pltpu.get_barrier_semaphore()
    partners = [sib, *y_to, z_up, z_dn, z_far, *x_to, x_two]
    for d in partners:
        pl.semaphore_signal(barrier, inc=1, device_id=d, device_id_type=MESH)

    @pl.when(jnp.logical_not(w_stays))
    def _():
        pl.semaphore_signal(barrier, inc=1, device_id=dev(p, x, z, core), device_id_type=MESH)

    for yy in range(4):
        @pl.when((x == p) & ((y != x) | (yy != y)))
        def _(yy=yy):
            pl.semaphore_signal(barrier, inc=1, device_id=dev(y, yy, z, core), device_id_type=MESH)

    for c in copies:
        c.wait()
    holds = jnp.where(x == p, 4, 0) + jnp.where(w_stays, -1, 1)
    pl.semaphore_wait(barrier, len(partners) + holds)

    def z_send(t):
        return rc(chunk(p - t, y, core), chunk(p - t, y, core), zs.at[t], zr.at[t + 1], z_up)

    def y_send(t, d):
        return rc(chunk(p - t, y, core), chunk(p - t, y, core), ys.at[d, t], yr.at[d, t], y_to[d])

    def y_got(t, d):
        c = chunk(p - t, (y + 3 - 2 * d) % 4, core)
        return rc(c, c, ys.at[d, t], yr.at[d, t], y_to[d])

    def y_next(t, d):
        c = half(p - t, (y + 3 - 2 * d) % 4, core, d)
        return rc(c, c, ys2.at[d, t], yr2.at[d, t], y_to[d])

    def y_far(t, d):
        c = half(p - t, (y + 2) % 4, core, d)
        return rc(c, c, ys2.at[d, t], yr2.at[d, t], y_to[d])

    def c_send(t, off):
        c = chunk(p - t, (y + off) % 4, core)
        return rc(c, c, cs.at[t, off], cr.at[t, off], sib)

    def c_got(t, off):
        c = chunk(p - t, (y + off) % 4, 1 - core)
        return rc(c, c, cs.at[t, off], cr.at[t, off], sib)

    filled = (p == 3) & (x == 3)

    def z_fill(n):
        c = chunk(2, (y + (3, 1, 2)[n]) % 4, core)
        return rc(c, c, zfs.at[n], zfr.at[n], z_up)

    def fill():
        @pl.when(p == 2)
        def _():
            z_fill(2).start()

        @pl.when((p == 2) & (x == 3))
        def _():
            for n in range(2):
                z_fill(n).start()

    def enter(t):
        @pl.when(p >= t)
        def _():
            if t > 0:
                c = chunk(p - t, y, core)
                rc(c, c, zs.at[t], zr.at[t], z_up).wait_recv()
            if t < 3:
                @pl.when(p < 3)
                def _():
                    z_send(t).start()
            c_send(t, 0).start()
            if t != 1:
                for d in range(2):
                    y_send(t, d).start()

        if t == 1:
            @pl.when((p >= 1) & jnp.logical_not(filled))
            def _():
                for d in range(2):
                    y_send(t, d).start()

    def onward(t):
        @pl.when((p >= t) & (jnp.logical_not(filled) | (t != 1)))
        def _():
            for d in range(2):
                y_got(t, d).wait_recv()

                @pl.when((p < 3) | (t != 1))
                def _(d=d):
                    y_next(t, d).start()

                c_send(t, 3 - 2 * d).start()

    def finish(t):
        @pl.when((p >= t) & ((p < 3) | (t != 1)))
        def _():
            for d in range(2):
                y_far(t, d).wait_recv()
            c_send(t, 2).start()

    def fill_take():
        @pl.when(filled)
        def _():
            for d in range(2):
                z_fill(d).wait_recv()
                c_send(1, 3 - 2 * d).start()

        @pl.when(p == 3)
        def _():
            z_fill(2).wait_recv()
            c_send(1, 2).start()

    def w_move():
        return rc(w_hbm, wbuf.at[x, core, y], wxs.at[0], wxr.at[y], dev(p, x, z, core))

    def w_order(i):
        return (i + 2 * (1 - zh)) % 4

    def wz_send(i, d):
        c = wbuf.at[y, core, w_order(i)]
        return rc(c, c, wzs.at[d, i], wzr.at[i], z_up if d == 0 else z_dn)

    def w_pass(i):
        c = wbuf.at[y, core, w_order(i)]

        @pl.when((x == p) & (y == x) & (w_order(i) == y))
        def _():
            w_local.wait()

        @pl.when((x == p) & ((y != x) | (w_order(i) != y)))
        def _():
            rc(c, c, wxs.at[0], wxr.at[w_order(i)], sib).wait_recv()

        @pl.when(x != p)
        def _():
            rc(c, c, wzs.at[0, i], wzr.at[i], sib).wait_recv()

        @pl.when((p >= x) & (p < 3))
        def _():
            wz_send(i, 0).start()

        @pl.when((p <= x) & (p > 0))
        def _():
            wz_send(i, 1).start()

    def w_pass_some(first, last):
        for i in range(first, last):
            w_pass(i)

    def w_take(i):
        c = wbuf.at[y, core, w_order(i)]
        rc(c, c, wzs.at[0, i], wzr.at[i], sib).wait_recv()

    def w_half(yy, c_, k):
        return wbuf.at[yy, c_, pl.ds(2 * ((1 - zh + k) % 2), 2)]

    def wy_send(k, d):
        c = w_half(y, core, k)
        return rc(c, c, wys.at[d, k], wyr.at[d, k], y_to[d])

    def wy_got(k, d):
        c = w_half((y + 3 - 2 * d) % 4, core, k)
        return rc(c, c, wys.at[d, k], wyr.at[d, k], y_to[d])

    def wy_next(k, d):
        c = wbuf.at[(y + 3 - 2 * d) % 4, core, 2 * ((1 - zh + k) % 2) + d]
        return rc(c, c, wys2.at[d, k], wyr2.at[d, k], y_to[d])

    def wy_far(k, d):
        c = wbuf.at[(y + 2) % 4, core, 2 * ((1 - zh + k) % 2) + d]
        return rc(c, c, wys2.at[d, k], wyr2.at[d, k], y_to[d])

    def wc(k, off, c_):
        c = w_half((y + off) % 4, c_, k)
        return rc(c, c, wcs.at[k, off], wcr.at[k, off], sib)

    def w_enter(k):
        for d in range(2):
            wy_send(k, d).start()
        wc(k, 0, core).start()

    def w_onward(k):
        for d in range(2):
            wy_got(k, d).wait_recv()
            wy_next(k, d).start()
            wc(k, 3 - 2 * d, core).start()

    def w_finish(k):
        for d in range(2):
            wy_far(k, d).wait_recv()
        wc(k, 2, core).start()

    def w_done(k):
        for off in range(4):
            wc(k, off, 1 - core).wait_recv()

    @pl.when(jnp.logical_not(w_stays))
    def _():
        w_move().start()

    enter(0)

    kvbuf[0:4] = jnp.zeros((4, 2, BLOCK, HEAD_DIM), jnp.bfloat16)

    def mask_step(n, carry):
        m, strip = n // 4, n % 4
        i = lax.broadcasted_iota(jnp.int32, (32, WIN), 0) + strip * 32
        j = lax.broadcasted_iota(jnp.int32, (32, WIN), 1)
        d = 4 * BLOCK + i - j
        b = jnp.where(d == 0, 0.0, NEG)
        for e in range(NS):
            b = jnp.where(d == slash[e, kv * GROUP + m] + 1, 0.0, b)
        sbias[m, pl.ds(pl.multiple_of(strip * 32, 32), 32), :] = b
        return carry

    lax.fori_loop(0, 16, mask_step, 0)

    @pl.when(((p == 0) & (x == 0)) | ((p == 3) & (x == 3)))
    def _():
        w_pass_some(0, 2)

    enter(1)

    @pl.when(((p == 0) & (x == 0)) | ((p == 3) & (x == 3)))
    def _():
        w_pass_some(2, 4)

    @pl.when((p == 1) & (x < 2))
    def _():
        w_pass_some(0, 4)

    @pl.when((p == 2) & (x >= 2))
    def _():
        w_pass_some(0, 2)

    onward(0)
    enter(2)

    @pl.when((p == 2) & (x >= 2))
    def _():
        w_pass_some(2, 4)

    @pl.when((p == 2) & (x < 2))
    def _():
        w_pass_some(0, 4)

    onward(1)
    finish(0)

    @pl.when((p == 1) & (x >= 2))
    def _():
        w_pass_some(0, 4)

    fill()
    enter(3)
    onward(2)
    finish(1)
    onward(3)

    @pl.when((p == 3) & (x < 3))
    def _():
        w_take(0)
        w_take(1)

    fill_take()
    w_late = (p == 0) & (x > 0)

    @pl.when(jnp.logical_not(w_late))
    def _():
        w_enter(0)

    finish(2)
    finish(3)

    @pl.when((p == 3) & (x < 3))
    def _():
        w_take(2)
        w_take(3)

    @pl.when(jnp.logical_not(w_late))
    def _():
        w_enter(1)

    for t in range(4):
        @pl.when(p >= t)
        def _(t=t):
            for off in range(4):
                c_got(t, off).wait_recv()

    q_copy.wait()
    wi = lax.broadcasted_iota(jnp.int32, (BLOCK, WIN), 0)
    wj = lax.broadcasted_iota(jnp.int32, (BLOCK, WIN), 1)
    lane = lax.broadcasted_iota(jnp.int32, (1, WIN), 1)

    def attend(r):
        rows = pl.ds(pl.multiple_of(r * BLOCK, BLOCK), BLOCK)
        here = 4 * seq + r
        kw = kvbuf[pl.ds(here, 5), 0].reshape(WIN, HEAD_DIM)
        vw = kvbuf[pl.ds(here, 5), 1].reshape(WIN, HEAD_DIM)
        vw = jnp.concatenate([vw, jnp.ones((WIN, HEAD_DIM), jnp.bfloat16)], axis=1)
        ones = jnp.ones((PICK, HEAD_DIM), jnp.bfloat16)
        bcol = here - 4 + lane // BLOCK
        alt = jnp.where((wj >= 4 * BLOCK) & (wi >= wj - 4 * BLOCK), 0.0, NEG)
        for m in range(GROUP):
            q = q_ref[rows, m * HEAD_DIM : (m + 1) * HEAD_DIM]
            oncol = bcol <= 0
            pb = [jnp.full((1, BLOCK), jnp.where(here > 0, 0.0, NEG), jnp.float32)]
            at = [4]
            for e in range(NV):
                b = vert[e, kv * GROUP + m] + 1
                oncol = oncol | (bcol == b)
                pb.append(jnp.full((1, BLOCK), jnp.where(b < here, 0.0, NEG), jnp.float32))
                at.append(4 + jnp.where(b < here, b, 0))
            kp = jnp.concatenate([kvbuf[a, 0] for a in at], axis=0)
            vp = jnp.concatenate([kvbuf[a, 1] for a in at], axis=0)
            sw = dot_t(q, kw) + jnp.where(oncol, alt, sbias[m])
            sp = dot_t(q, kp) + jnp.concatenate(pb, axis=1)
            peak = jnp.maximum(
                jnp.max(sw, axis=1, keepdims=True), jnp.max(sp, axis=1, keepdims=True)
            )
            pw = jnp.exp2((sw - peak) * SCALE).astype(jnp.bfloat16)
            pp = jnp.exp2((sp - peak) * SCALE).astype(jnp.bfloat16)
            o = dot(pw, vw) + dot(pp, jnp.concatenate([vp, ones], axis=1))
            abuf[x, r, m] = (o[:, :HEAD_DIM] / o[:, HEAD_DIM:]).astype(jnp.bfloat16)

    def a_part(xx, r, m):
        return abuf.at[xx, r, pl.ds(m - UNIT + 1, UNIT)]

    def x_copy(c, ss, rs, r, m, d):
        n = r * GROUP + m
        return rc(c, c, ss.at[d, n], rs.at[d, n], x_to[d])

    def x_send(r, m, d):
        return x_copy(a_part(x, r, m), xs, xr, r, m, d)

    def x_got(r, m, d):
        return x_copy(a_part((x + 3 - 2 * d) % 4, r, m), xs, xr, r, m, d)

    def x_far(xx, r, m):
        c = a_part(xx, r, m)
        n = r * GROUP + m
        return rc(c, c, xs2.at[n], xr2.at[n], x_two)

    def e_send(r, d):
        c = pl.ds(d * 64, 64)
        return rc(zsrc.at[r, c], zdst.at[r, c], es.at[d, r], er.at[d, r], z_far)

    def product(r, h):
        acc = None
        for i in range(4):
            w = jnp.concatenate(
                [wbuf[i, n % 2, 2 * h + n // 2] for n in range(4)], axis=1
            )
            a = jnp.concatenate([abuf[i, r, m] for m in range(GROUP)], axis=1)
            part = dot(a, w)
            acc = part if acc is None else acc + part
        return acc

    ends = range(UNIT - 1, GROUP, UNIT)

    def step(it, carry):
        @pl.when(it < RBLK)
        def _():
            attend(it)
            for m in ends:
                for d in range(2):
                    x_send(it, m, d).start()
                x_far(x, it, m).start()

        @pl.when((it == LATE) & w_late)
        def _():
            w_take(0)
            w_take(1)
            w_enter(0)
            w_take(2)
            w_take(3)
            w_enter(1)

        for at, act, k in W_STEPS:
            @pl.when(it == at)
            def _(act=act, k=k):
                (w_onward, w_finish, w_done)[act](k)

        @pl.when((it >= LAG2) & (it < RBLK + LAG2))
        def _():
            r = it - LAG2
            for m in ends:
                for d in range(2):
                    x_got(r, m, d).wait_recv()
                x_far((x + 2) % 4, r, m).wait_recv()
            zsrc[r] = product(r, 1 - zh).astype(jnp.bfloat16)
            for d in range(2):
                e_send(r, d).start()

        for at, act, k in W_LATER:
            @pl.when(it == at)
            def _(act=act, k=k):
                (w_onward, w_finish, w_done)[act](k)

        @pl.when(it >= LAG3)
        def _():
            r = it - LAG3
            mine = product(r, zh)
            for d in range(2):
                e_send(r, d).wait_recv()
            rows = pl.ds(pl.multiple_of(r * BLOCK, BLOCK), BLOCK)
            out_ref[rows, :] = (mine + zdst[r].astype(jnp.float32)).astype(jnp.bfloat16)

        return carry

    lax.fori_loop(0, RBLK + LAG3, step, 0)

    for t in range(4):
        @pl.when(p >= t)
        def _(t=t):
            if t < 3:
                @pl.when(p < 3)
                def _():
                    z_send(t).wait_send()
            for off in range(4):
                c_send(t, off).wait_send()

        @pl.when((p >= t) & (jnp.logical_not(filled) | (t != 1)))
        def _(t=t):
            for d in range(2):
                y_send(t, d).wait_send()

        @pl.when((p >= t) & ((p < 3) | (t != 1)))
        def _(t=t):
            for d in range(2):
                y_next(t, d).wait_send()

    @pl.when(p == 2)
    def _():
        z_fill(2).wait_send()

    @pl.when((p == 2) & (x == 3))
    def _():
        for n in range(2):
            z_fill(n).wait_send()

    @pl.when(jnp.logical_not(w_stays))
    def _():
        w_move().wait_send()

    for i in range(4):
        @pl.when((p >= x) & (p < 3))
        def _(i=i):
            wz_send(i, 0).wait_send()

        @pl.when((p <= x) & (p > 0))
        def _(i=i):
            wz_send(i, 1).wait_send()

    for k in range(2):
        for d in range(2):
            wy_send(k, d).wait_send()
            wy_next(k, d).wait_send()
        for off in range(4):
            wc(k, off, core).wait_send()

    def drain(r, carry):
        for d in range(2):
            for m in range(UNIT - 1, GROUP, UNIT):
                x_send(r, m, d).wait_send()
            e_send(r, d).wait_send()
        for m in ends:
            x_far(x, r, m).wait_send()
        return carry

    lax.fori_loop(0, 4, drain, 0)


def shards(queries, key_rows, value_rows, out_weight, vertical, slash_offsets):
    bf16 = jnp.bfloat16
    dma = pltpu.SemaphoreType.DMA
    smem = pl.BlockSpec(memory_space=pltpu.SMEM)
    vmem = pl.BlockSpec(memory_space=pltpu.VMEM)
    anyspace = pl.BlockSpec(memory_space=pl.ANY)
    return pl.pallas_call(
        kernel,
        out_shape=jax.ShapeDtypeStruct((ROWS, ROWS), bf16),
        in_specs=[smem, smem, anyspace, anyspace, anyspace, anyspace],
        out_specs=vmem,
        scratch_shapes=[
            pltpu.VMEM((ROWS, GROUP * HEAD_DIM), bf16),
            pltpu.VMEM((132, 2, BLOCK, HEAD_DIM), bf16),
            pltpu.VMEM((4, 2, 4, ROWS, 128), bf16),
            pltpu.VMEM((4, RBLK, GROUP, BLOCK, HEAD_DIM), bf16),
            pltpu.VMEM((GROUP, BLOCK, WIN), jnp.float32),
            pltpu.VMEM((RBLK, BLOCK, ROWS), bf16),
            pltpu.VMEM((RBLK, BLOCK, ROWS), bf16),
            dma((4,)),
            dma((4,)), dma((4,)), dma((3,)), dma((3,)),
            dma((2, 4)), dma((2, 4)), dma((2, 4)), dma((2, 4)),
            dma((4, 4)), dma((4, 4)),
            dma((1,)), dma((4,)),
            dma((2, 4)), dma((4,)),
            dma((2, 2)), dma((2, 2)), dma((2, 2)), dma((2, 2)),
            dma((2, 4)), dma((2, 4)),
            dma((2, 16)), dma((2, 16)), dma((16,)), dma((16,)),
            dma((2, 4)), dma((2, 4)),
        ],
        compiler_params=pltpu.CompilerParams(
            collective_id=0, has_side_effects=True, vmem_limit_bytes=56 * 1024 * 1024
        ),
    )(
        vertical.T,
        slash_offsets.T,
        queries,
        key_rows.reshape(4, BLOCK, HEAD_DIM),
        value_rows.reshape(4, BLOCK, HEAD_DIM),
        out_weight,
    )


def solution(mesh):
    in_specs = (P("seq", "kv"), P("seq", "kv"), P("seq", "kv"), P("kv", "seq"), P(), P())
    out_specs = P("seq", "kv")
    return jax.shard_map(shards, mesh=mesh, in_specs=in_specs, out_specs=out_specs, check_vma=False)
```
